32 devices in a mesh: grp: 2 (over x), rel: 16 (over z, y, core).
Axes of the slice: x: 2, y: 2, z: 4, core: 2. Of those that a mesh axis runs over, the one named last changes fastest.
Arguments:
- coarse: float32 [196608], P(('grp', 'rel')), parts along dimension 0, may hold values from -1 to 1
- background: float32 [4, 256, 256], P('grp'), parts along dimension 0, may hold values from 0 to 2
- sources: int32 [32], P(('grp', 'rel')), parts along dimension 0, may hold values from 0 to 131071, as said below
- durations: int32 [32], P(('grp', 'rel')), parts along dimension 0, may hold values from 1 to 6
- counts: int32 [32], P(('grp', 'rel')), parts along dimension 0, may hold values from 1 to 6
- sensors: int32 [32, 64], P(('grp', 'rel')), parts along dimension 0, may hold values from 0 to 131071, as said below
- observed: float32 [32, 64], P(('grp', 'rel')), parts along dimension 0, may hold values from -5 to 5
Outputs:
- direction: float32 [196608], P(('grp', 'rel')), parts along dimension 0
- misfit: float32 [32], P(('grp', 'rel')), parts along dimension 0
The draws below stay inside these ranges and needn't reach their ends.
There are 2 independent parts, one for each index of `grp`. The reference program is written for one: setup_inputs(seed, part) draws one part's arguments, and reference() takes and returns one part's arrays. A program takes and returns all parts, laid end to end along the dimension named above; each array names one. Nothing has to cross between parts.
Inputs may be any that keep to these rules, and one draw needn't show every extreme that they name: `sources`: A flat cell index level * 256 * 256 + x * 256 + y. Flat cell indices like sources; half of a release's sensors lie within 3 cells horizontally of its source, on its level.
All inputs are finite; a program needn't handle non-finite values.
Results may differ from the reference program's by a relative error of at most 0.0003.
Values sent between devices are 32-bit elements; how exact they have to be, the bound alone decides.
No kernel may reach another device: no remote copies, remote signals or barrier semaphores. Data moves between devices by JAX's collectives and lax.ppermute only.
A program may use at most 64 MiB of HBM per device.

```python
import jax
import jax.numpy as jnp
from jax import lax

NX = 256
NY = 256
NZ = 2
STEPS = 6
NSENS = 64
RELEASES = 16
NCOARSE = 98304


def placement_helper(key):
    base = jax.random.fold_in(key, 17)
    keys = jax.random.split(base, 6)
    level = jax.random.randint(keys[0], (RELEASES,), 0, NZ)
    column = jax.random.randint(keys[1], (RELEASES,), 0, NX)
    row_pos = jax.random.randint(keys[2], (RELEASES,), 0, NY)
    source = level * NX * NY + column * NY + row_pos
    near_count = NSENS // 2
    far_count = NSENS - near_count
    shift_x = jax.random.randint(keys[3], (RELEASES, near_count), -3, 4)
    shift_y = jax.random.randint(keys[4], (RELEASES, near_count), -3, 4)
    near_x = jnp.clip(column[:, None] + shift_x, 0, NX - 1)
    near_y = jnp.clip(row_pos[:, None] + shift_y, 0, NY - 1)
    near = level[:, None] * NX * NY + near_x * NY + near_y
    far = jax.random.randint(keys[5], (RELEASES, far_count), 0, NZ * NX * NY)
    sensor = jnp.concatenate([near, far], axis=1)
    return (source.astype(jnp.int32), sensor.astype(jnp.int32))


def draw_sources(key, part):
    return placement_helper(key)[0]


def draw_sensors(key, part):
    return placement_helper(key)[1]


def touch_ends(drawn, stream_key, smallest, largest):
    dims = drawn.shape
    spot = [jax.random.randint(jax.random.fold_in(stream_key, axis), (), 0, dims[axis]) for axis in range(len(dims))]
    drawn = drawn.at[tuple(spot)].set(smallest)
    longest = dims.index(max(dims))
    spot[longest] = (spot[longest] + 1) % dims[longest]
    return drawn.at[tuple(spot)].set(largest)


def shard_levels(own_key, dims, pieces, smallest, top_value):
    factor_of = 1.0
    for axis_at, parts in pieces:
        heights = jax.random.uniform(jax.random.fold_in(jax.random.fold_in(own_key, 6), axis_at), (parts,), jnp.float32, smallest / len(pieces), top_value / len(pieces))
        factor_of = factor_of * jnp.repeat(jnp.exp(heights), dims[axis_at] // parts).reshape((-1,) + (1,) * (len(dims) - 1 - axis_at))
    return factor_of


def scatter_about(own_key, shape, deviation, bound, cuts=(), dtype=jnp.bfloat16):
    entries = deviation * jax.random.normal(own_key, shape, jnp.float32)
    if cuts:
        entries = entries * shard_levels(own_key, shape, cuts, -0.22, 0.18)
    return jnp.clip(entries, -bound, bound).astype(dtype)


def setup_inputs(seed: int = 0, part: int = 0) -> dict:
    splits = jax.random.split(jax.random.key(seed), 8)
    own_keys = jax.random.split(jax.random.fold_in(splits[7], part), 8)
    coarse = jnp.clip(jax.random.uniform(own_keys[0], (NCOARSE,), jnp.float32, -1.0, 1.0) * shard_levels(own_keys[0], (NCOARSE,), ((0, 16),), -0.4, 0.0), -1.0, 1.0)
    background = jnp.clip(jax.random.uniform(own_keys[1], (NZ, NX, NY), jnp.float32, 0.0, 2.0), 0.0, 2.0)
    sources = draw_sources(jax.random.fold_in(jax.random.fold_in(splits[7], part), 71), part)
    durations = touch_ends(jax.random.randint(own_keys[3], (RELEASES,), 1, STEPS + 1), jax.random.fold_in(own_keys[3], 1), 1, STEPS).astype(jnp.int32)
    counts = touch_ends(jax.random.randint(own_keys[4], (RELEASES,), 1, STEPS + 1), jax.random.fold_in(own_keys[4], 1), 1, STEPS).astype(jnp.int32)
    sensors = draw_sensors(jax.random.fold_in(jax.random.fold_in(splits[7], part), 71), part)
    observed = scatter_about(own_keys[6], (RELEASES, NSENS), 1.0, 5.0, ((0, 16),), jnp.float32)
    return dict(coarse=coarse, background=background, sources=sources, durations=durations, counts=counts, sensors=sensors, observed=observed)


def prolong(params):
    fields = params.reshape(3, NZ, NX // 2, NY // 2)
    fine = jnp.repeat(jnp.repeat(fields, 2, axis=2), 2, axis=3)
    diffusivity = 0.05 * jnp.exp(fine[0])
    wind_x = 0.08 * jnp.tanh(fine[1])
    wind_y = 0.08 * jnp.tanh(fine[2])
    return (diffusivity, wind_x, wind_y)

def advance(concentration, diffusivity, wind_x, wind_y, source, emission, live):
    padded = jnp.pad(concentration, 1)
    cell_west = padded[1:-1, :-2, 1:-1]
    cell_east = padded[1:-1, 2:, 1:-1]
    cell_south = padded[1:-1, 1:-1, :-2]
    cell_north = padded[1:-1, 1:-1, 2:]
    cell_below = padded[:-2, 1:-1, 1:-1]
    cell_above = padded[2:, 1:-1, 1:-1]
    spread = diffusivity * (cell_west + cell_east + cell_south + cell_north + cell_below + cell_above - 6.0 * concentration)
    carried = jnp.maximum(wind_x, 0.0) * (concentration - cell_west) + jnp.minimum(wind_x, 0.0) * (cell_east - concentration)
    carried = carried + jnp.maximum(wind_y, 0.0) * (concentration - cell_south) + jnp.minimum(wind_y, 0.0) * (cell_north - concentration)
    candidate = concentration + spread - carried
    candidate = candidate.reshape(-1).at[source].add(emission).reshape(concentration.shape)
    return jnp.where(live, candidate, concentration)

def release_loss(params, background, source, duration, count, sensor, observed):
    diffusivity, wind_x, wind_y = prolong(params)
    concentration = background
    for instant in range(STEPS):
        emission = 4.0 * jnp.logical_and(instant < duration, instant < count).astype(jnp.float32)
        concentration = advance(concentration, diffusivity, wind_x, wind_y, source, emission, instant < count)
    sampled = concentration.reshape(-1)[sensor]
    return 0.5 * jnp.sum((sampled - observed) ** 2)

def reference(coarse, background, sources, durations, counts, sensors, observed):

    def single(record):
        source, duration, count, sensor, watched = record
        value, pullback = jax.vjp(lambda params: release_loss(params, background, source, duration, count, sensor, watched), coarse)
        slope, = pullback(jnp.ones_like(value))
        return (value / NSENS, slope)
    misfit, slopes = lax.map(single, (sources, durations, counts, sensors, observed))
    gradient = lax.optimization_barrier(jnp.sum(slopes, axis=0))
    direction = gradient / jnp.sqrt(jnp.mean(gradient * gradient) + 1e-06)
    return (direction, misfit)
```

```python
import functools

import jax
import jax.numpy as jnp
from jax import lax
from jax.experimental import pallas as pl
from jax.experimental.pallas import tpu as pltpu
from jax.sharding import PartitionSpec as P

STEPS = 6
NSENS = 64
PAD = 8
BATCH = 32
SLOTS = 16
ROWS = 128
LANES = 128
PLANE = ROWS + 2 * PAD
FIELD = 8 * PLANE
VMEM_LIMIT = 40 * 1024 * 1024
F32, BF16, I32 = jnp.float32, jnp.bfloat16, jnp.int32


def loop(first, end, unroll=1):
    def run(body):
        lax.fori_loop(first, end, body, None, unroll=unroll)

    return run


def plane_at(z, px, py):
    return ((z * 2 + px) * 2 + py) * PLANE + PAD


def split(value):
    high = value.astype(BF16)
    return high, (value - high.astype(F32)).astype(BF16)


def pack_kernel(coarse_ref, sensors_ref, observed_ref, source_ref, duration_ref, count_ref, out_ref):
    rows = coarse_ref.shape[0]
    out_ref[...] = jnp.zeros_like(out_ref)
    out_ref[pl.ds(0, rows), :] = coarse_ref[...]
    out_ref[pl.ds(rows, 1), pl.ds(0, NSENS)] = sensors_ref[...].astype(F32)
    out_ref[pl.ds(rows, 1), pl.ds(NSENS, NSENS)] = observed_ref[...]
    lane = lax.broadcasted_iota(I32, (1, LANES), 1)
    record = jnp.where(lane == 0, source_ref[0], jnp.where(lane == 1, duration_ref[0], count_ref[0]))
    out_ref[pl.ds(rows + 1, 1), :] = record.astype(F32)


def planes_kernel(background_ref, out_ref, half_ref):
    width = background_ref.shape[2]
    out_ref[...] = jnp.zeros_like(out_ref)
    column = lax.broadcasted_iota(I32, (width, width), 1)
    row = lax.broadcasted_iota(I32, (width, width), 0)
    wanted = jnp.where(column < LANES, 2 * column, 2 * (column - LANES) + 1)
    pick = (row == wanted).astype(F32)
    for z in range(2):
        sorted_lanes = jnp.dot(
            background_ref[z], pick, precision=lax.Precision.HIGHEST, preferred_element_type=F32
        )
        for py in range(2):
            half_ref[z * 2 + py] = sorted_lanes[:, py * LANES : (py + 1) * LANES]
            for px in range(2):
                out_ref[pl.ds(plane_at(z, px, py), ROWS), :] = half_ref[z * 2 + py, pl.ds(px, ROWS, stride=2), :]


def gradient_kernel(
    order,
    rows,
    first_ref,
    second_ref,
    planes_ref,
    direction_ref,
    misfit_ref,
    par,
    coef,
    hist,
    lam_a,
    lam_b,
    acc,
    grad,
    sens_rows,
    meta_rows,
    table,
    gathered,
    scattered,
    scalars,
    sem,
):
    blocks = len(order)
    block = first_ref.shape[0] // (blocks // 2)
    me = lax.axis_index("rel")
    groups = -(-blocks // SLOTS)
    lane = lax.broadcasted_iota(I32, (8, LANES), 1)
    sub = lax.broadcasted_iota(I32, (8, LANES), 0)

    par[pl.ds(0, 8), :] = jnp.zeros((8, LANES), F32)
    par[pl.ds(8 + 6 * ROWS, 8), :] = jnp.zeros((8, LANES), F32)
    for p in range(blocks):
        ref = first_ref if p < blocks // 2 else second_ref
        at = (p % (blocks // 2)) * block
        owner = me ^ order[p]
        if rows % 8 == 0:
            place = pl.multiple_of(owner * rows + 8, 8)
        else:
            place = owner * rows + 8
        par[pl.ds(place, rows), :] = ref[pl.ds(at, rows), :]
        sens_rows[pl.ds(owner, 1), :] = ref[pl.ds(at + rows, 1), :]
        meta_rows[pl.ds(owner, 1), :] = ref[pl.ds(at + rows + 1, 1), :]

    wide = lax.broadcasted_iota(I32, (blocks, LANES), 1)
    release = lax.broadcasted_iota(I32, (blocks, LANES), 0)
    sens = jnp.where(wide < NSENS, sens_rows[...], 0.0).astype(I32)
    meta = meta_rows[...].astype(I32)
    source = jnp.broadcast_to(meta[:, 0:1], (blocks, LANES))
    duration = jnp.broadcast_to(meta[:, 1:2], (blocks, LANES))
    count = jnp.broadcast_to(meta[:, 2:3], (blocks, LANES))
    fine_x, fine_y = (sens >> 8) & 255, sens & 255
    plane = (sens >> 16) * 4 + (fine_x & 1) * 2 + (fine_y & 1)
    cell_x, cell_y = fine_x >> 1, fine_y >> 1
    left_x = (((source >> 8) & 255) >> 1) - 3
    left_y = ((source & 255) >> 1) - 3
    off_x, off_y = cell_x - left_x, cell_y - left_y
    inside = (off_x >= 0) & (off_x < 8) & (off_y >= 0) & (off_y < 8)
    patch_row = jnp.where(inside, plane * 8 + off_x, -1)
    patch_lane = jnp.where(inside, (release % SLOTS) * 8 + off_y, -1)
    address = (count - 1) * FIELD + plane * PLANE + PAD + cell_x
    row_id = (plane * ROWS + cell_x).astype(F32)
    for at, value in ((0, source), (1, duration), (2, count), (3, left_x), (4, left_y)):
        address = jnp.where(wide == NSENS + at, value, address)
    table[...] = address
    copy = pltpu.make_async_copy(table, scalars, sem)
    copy.start()

    names = ("centre", "east", "west", "north", "south", "diff", "south0", "north1", "northr", "southl", "wx", "wy", "fx", "fy")
    index = {name: i for i, name in enumerate(names)}

    def coef_at(name, z, x):
        return pl.ds((index[name] * 2 + z) * PLANE + PAD + x, 8)

    zeros = jnp.zeros((8, LANES), F32)
    for z in range(2):
        coef[coef_at("east", z, -8), :] = zeros
        coef[coef_at("west", z, ROWS), :] = zeros

    def coefficients(p0, p1, p2):
        diff = 0.05 * jnp.exp(p0)
        t1, t2 = jnp.tanh(p1), jnp.tanh(p2)
        wx, wy = 0.08 * t1, 0.08 * t2
        east, west = diff - jnp.minimum(wx, 0.0), diff + jnp.maximum(wx, 0.0)
        north, south = diff - jnp.minimum(wy, 0.0), diff + jnp.maximum(wy, 0.0)
        centre = 1.0 - (east + west + north + south + 2.0 * diff)
        return dict(
            centre=centre, east=east, west=west, north=north, south=south, diff=diff,
            wx=wx, wy=wy, fx=0.08 * (1.0 - t1 * t1), fy=0.08 * (1.0 - t2 * t2),
        )

    @loop(0, ROWS // 8, unroll=4)
    def _(i, carry):
        x = pl.multiple_of(i * 8, 8)
        for z in range(2):
            p0, p1, p2 = (par[pl.ds((f * 2 + z) * ROWS + 8 + x, 8), :] for f in range(3))
            made = coefficients(p0, p1, p2)
            made["south0"] = jnp.where(lane == 0, 0.0, made["south"])
            made["north1"] = jnp.where(lane == LANES - 1, 0.0, made["north"])
            made["northr"] = jnp.where(lane == 0, 0.0, pltpu.roll(made["north"], 1, 1))
            made["southl"] = jnp.where(lane == LANES - 1, 0.0, pltpu.roll(made["south"], LANES - 1, 1))
            for name, value in made.items():
                coef[coef_at(name, z, x), :] = value
        return carry

    for p in range(8):
        for ref, fields in ((hist, STEPS), (lam_a, 1), (lam_b, 1)):
            for f in range(fields):
                ref[pl.ds(f * FIELD + p * PLANE, 8), :] = zeros
                ref[pl.ds(f * FIELD + p * PLANE + PAD + ROWS, 8), :] = zeros

    def load(ref, base, x):
        def at(z, px, py, shift=0):
            return ref[pl.ds(base + plane_at(z, px, py) + x + shift, 8), :]

        own = [[[at(z, px, py) for py in range(2)] for px in range(2)] for z in range(2)]
        odd = [[at(z, 1, py, -1) for py in range(2)] for z in range(2)]
        even = [[at(z, 0, py, 1) for py in range(2)] for z in range(2)]
        return own, odd, even

    def forward(src, src_base, dst, dst_base):
        @loop(0, ROWS // 8, unroll=2)
        def _(i, carry):
            x = pl.multiple_of(i * 8, 8)
            own, odd, even = load(src, src_base, x)
            for z in range(2):
                k = {
                    name: coef[coef_at(name, z, x), :]
                    for name in ("centre", "east", "west", "north", "south", "diff", "south0", "north1")
                }
                for px in range(2):
                    c0, c1 = own[z][px]
                    along_y = (
                        k["north"] * c1 + k["south0"] * pltpu.roll(c1, 1, 1),
                        k["north1"] * pltpu.roll(c0, LANES - 1, 1) + k["south"] * c0,
                    )
                    for py in range(2):
                        if px == 0:
                            along_x = k["east"] * own[z][1][py] + k["west"] * odd[z][py]
                        else:
                            along_x = k["east"] * even[z][py] + k["west"] * own[z][0][py]
                        new = (k["centre"] * own[z][px][py] + along_x) + (
                            along_y[py] + k["diff"] * own[1 - z][px][py]
                        )
                        dst[pl.ds(dst_base + plane_at(z, px, py) + x, 8), :] = new
            return carry

    forward(planes_ref, 0, hist, 0)
    for t in range(1, STEPS):
        forward(hist, (t - 1) * FIELD, hist, t * FIELD)

    copy.wait()

    @loop(0, blocks)
    def _(r, carry):
        to = pl.multiple_of(r * NSENS, NSENS)
        for s in range(NSENS):
            gathered[pl.ds(to + s, 1), :] = hist[pl.ds(scalars[r, s], 1), :]
        return carry

    slot = lane >> 3
    patches = []
    for g in range(groups):
        members = range(g * SLOTS, min(blocks, (g + 1) * SLOTS))
        pp = [[zeros, zeros] for _ in range(3)]
        at_x, at_y, of_plane, lasts, emits = (jnp.zeros((8, LANES), I32) for _ in range(5))
        for r in members:
            here = slot == r % SLOTS
            src, dur, cnt = scalars[r, NSENS], scalars[r, NSENS + 1], scalars[r, NSENS + 2]
            x0, y0 = scalars[r, NSENS + 3], scalars[r, NSENS + 4]
            shift = (8 * (r % SLOTS) - y0) & (LANES - 1)
            for f in range(3):
                for z in range(2):
                    window = par[pl.ds((f * 2 + z) * ROWS + 8 + x0, 8), :]
                    pp[f][z] = jnp.where(here, pltpu.roll(window, shift, 1), pp[f][z])
            src_plane = (src >> 16) * 4 + ((src >> 8) & 1) * 2 + (src & 1)
            at_x = jnp.where(here, x0, at_x)
            at_y = jnp.where(here, y0, at_y)
            of_plane = jnp.where(here, src_plane, of_plane)
            emits = jnp.where(here, dur, emits)
            lasts = jnp.where(here, cnt, lasts)
        in_x, in_y = at_x + sub, at_y + (lane & 7)
        valid = (in_x >= 0) & (in_x < ROWS) & (in_y >= 0) & (in_y < LANES)
        ks = []
        for z in range(2):
            made = coefficients(pp[0][z], pp[1][z], pp[2][z])
            ks.append({name: jnp.where(valid, value, 0.0) for name, value in made.items()})
        spot = (sub == 3) & ((lane & 7) == 3)
        state = [[[zeros for _ in range(2)] for _ in range(2)] for _ in range(2)]
        plume = []
        for t in range(STEPS):
            plume.append(state)
            new = [[[None, None], [None, None]], [[None, None], [None, None]]]
            for z in range(2):
                k = ks[z]
                for px in range(2):
                    for py in range(2):
                        c = state[z][px][py]
                        other_x, other_y = state[z][1 - px][py], state[z][px][1 - py]
                        if px == 0:
                            along_x = k["east"] * other_x + k["west"] * pltpu.roll(other_x, 1, 0)
                        else:
                            along_x = k["east"] * pltpu.roll(other_x, 7, 0) + k["west"] * other_x
                        if py == 0:
                            along_y = k["north"] * other_y + k["south"] * pltpu.roll(other_y, 1, 1)
                        else:
                            along_y = k["north"] * pltpu.roll(other_y, LANES - 1, 1) + k["south"] * other_y
                        value = (k["centre"] * c + along_x) + (along_y + k["diff"] * state[1 - z][px][py])
                        emit = spot & (of_plane == z * 4 + px * 2 + py) & (t < emits)
                        value = value + jnp.where(emit, 4.0, 0.0)
                        new[z][px][py] = jnp.where(t < lasts, value, c)
            state = new
        patches.append((ks, valid, lasts, plume, state))

    lane_f, row_f = patch_lane.astype(F32), patch_row.astype(F32)
    first_half = wide < NSENS
    turn_a = jnp.where(first_half, cell_y.astype(F32), pltpu.roll(lane_f, NSENS, 1)).T
    turn_b = jnp.where(first_half, row_f, pltpu.roll(row_id, NSENS, 1)).T
    turn_c = sens_rows[...].T
    lane64 = lax.broadcasted_iota(I32, (NSENS, LANES), 1).astype(F32)
    lane_sq = lax.broadcasted_iota(I32, (NSENS, NSENS), 1).astype(F32)
    sub_sq = lax.broadcasted_iota(I32, (NSENS, NSENS), 0).astype(F32)
    batch = (lane_sq.astype(I32) // BATCH) == (sub_sq.astype(I32) // BATCH)
    loss = jnp.zeros((NSENS, LANES), F32)
    seeds = []
    for g in range(groups):
        members = range(g * SLOTS, min(blocks, (g + 1) * SLOTS))
        final = patches[g][4]
        flat = jnp.concatenate([final[z][px][py] for z in range(2) for px in range(2) for py in range(2)], axis=0)
        flat = jnp.concatenate(split(flat), axis=1)
        seed = jnp.zeros((NSENS, 2 * LANES), F32)
        for r in members:
            def column(turned, half):
                return jnp.broadcast_to(turned[half * NSENS : (half + 1) * NSENS, r : r + 1], (NSENS, LANES))

            own_lane, own_patch = column(turn_a, 0), column(turn_a, 1)
            own_row, own_cell = column(turn_b, 0), column(turn_b, 1)
            watched = column(turn_c, 1)
            pick = (own_row[:, :NSENS] == lane_sq).astype(BF16)
            near = jnp.dot(pick, flat, preferred_element_type=F32)
            near = near[:, :LANES] + near[:, LANES:]
            on_lane, on_patch = lane64 == own_lane, lane64 == own_patch
            value = jnp.where(on_lane, gathered[pl.ds(r * NSENS, NSENS), :], 0.0)
            value = value + jnp.where(on_patch, near, 0.0)
            residual = jnp.sum(value, axis=1, keepdims=True) - watched
            loss = jnp.where(me == r, residual * residual, loss)
            same = own_cell[:, :NSENS] == jnp.broadcast_to(row_id[r : r + 1, :NSENS], (NSENS, NSENS))
            same = (same & batch).astype(BF16)
            spread = jnp.dot(
                same,
                jnp.concatenate(split(jnp.where(on_lane, residual, 0.0)), axis=1),
                preferred_element_type=F32,
            )
            scattered[pl.ds(r * NSENS, NSENS), :] = spread[:, :LANES] + spread[:, LANES:]
            put = (sub_sq == jnp.broadcast_to(row_f[r : r + 1, :NSENS], (NSENS, NSENS))).astype(BF16)
            seed = seed + jnp.dot(
                put,
                jnp.concatenate(split(jnp.where(on_patch, residual, 0.0)), axis=1),
                preferred_element_type=F32,
            )
        seed = seed[:, :LANES] + seed[:, LANES:]
        seeds.append(
            [[[seed[((z * 2 + px) * 2 + py) * 8 :][:8] for py in range(2)] for px in range(2)] for z in range(2)]
        )
    misfit_ref[0] = jnp.sum(loss[:, 0:1]) * (0.5 / NSENS)

    def seed_sensors(ref, t):
        @loop(0, blocks)
        def _(r, carry):
            @pl.when(scalars[r, NSENS + 2] == t)
            def _():
                at = pl.multiple_of(r * NSENS, NSENS)
                for part in range(0, NSENS, BATCH):
                    spots, news = [], []
                    for s in range(part, part + BATCH):
                        spot = pl.ds(scalars[r, s] - (t - 1) * FIELD, 1)
                        spots.append(spot)
                        news.append(ref[spot, :] + scattered[pl.ds(at + s, 1), :])
                    for spot, new in zip(spots, news):
                        ref[spot, :] = new

            return carry

    def acc_at(q, z, x):
        return pl.ds((q * 2 + z) * ROWS + x, 8)

    def backward(src, dst, conc, conc_base, first, last):
        @loop(0, ROWS // 8, unroll=2)
        def _(i, carry):
            x = pl.multiple_of(i * 8, 8)
            lam, lam_odd, lam_even = load(src, 0, x)
            own, odd, even = load(conc, conc_base, x)
            diffs = [coef[coef_at("diff", z, x), :] for z in range(2)]
            for z in range(2):
                if not last:
                    k = {
                        name: coef[coef_at(name, z, x), :]
                        for name in ("centre", "east", "west", "north", "south", "northr", "southl")
                    }
                    east_m, west_p = coef[coef_at("east", z, x - 1), :], coef[coef_at("west", z, x + 1), :]
                    for px in range(2):
                        l0, l1 = lam[z][px]
                        along_y = (
                            k["south"] * l1 + k["northr"] * pltpu.roll(l1, 1, 1),
                            k["southl"] * pltpu.roll(l0, LANES - 1, 1) + k["north"] * l0,
                        )
                        for py in range(2):
                            if px == 0:
                                along_x = k["west"] * lam[z][1][py] + east_m * lam_odd[z][py]
                            else:
                                along_x = west_p * lam_even[z][py] + k["east"] * lam[z][0][py]
                            new = (k["centre"] * lam[z][px][py] + along_x) + (
                                along_y[py] + diffs[1 - z] * lam[1 - z][px][py]
                            )
                            dst[pl.ds(plane_at(z, px, py) + x, 8), :] = new
                sums = [None] * 5
                for px in range(2):
                    c0, c1 = own[z][px]
                    mid = c1 - c0
                    to_north = (mid, jnp.where(lane == LANES - 1, 0.0, pltpu.roll(c0, LANES - 1, 1)) - c1)
                    to_south = (c0 - jnp.where(lane == 0, 0.0, pltpu.roll(c1, 1, 1)), mid)
                    for py in range(2):
                        c, l = own[z][px][py], lam[z][px][py]
                        mid_x = own[z][1][py] - own[z][0][py]
                        if px == 0:
                            to_east, to_west = mid_x, c - odd[z][py]
                        else:
                            to_east, to_west = even[z][py] - c, mid_x
                        rise = own[1 - z][px][py] - 2.0 * c
                        for q, d in enumerate((to_east, to_west, to_north[py], to_south[py], rise)):
                            term = l * d
                            sums[q] = term if sums[q] is None else sums[q] + term
                for q in range(5):
                    at = acc_at(q, z, x)
                    acc[at, :] = sums[q] if first else acc[at, :] + sums[q]
            return carry

    @loop(0, FIELD // 64)
    def _(i, carry):
        lam_a[pl.ds(pl.multiple_of(i * 64, 64), 64), :] = jnp.zeros((64, LANES), F32)
        return carry

    src, dst = lam_a, lam_b
    for t in range(STEPS - 1, -1, -1):
        seed_sensors(src, t + 1)
        if t == 0:
            backward(src, dst, planes_ref, 0, False, True)
        else:
            backward(src, dst, hist, (t - 1) * FIELD, t == STEPS - 1, False)
        src, dst = dst, src

    def chain(sums, diff, wx, wy, fx, fy):
        to_east, to_west, to_north, to_south, rise = sums

        def wind(w, up, down, factor):
            plus = jnp.where(w > 0.0, 1.0, jnp.where(w == 0.0, 0.5, 0.0))
            return -(plus * up + (1.0 - plus) * down) * factor

        g0 = (to_east - to_west + to_north - to_south + rise) * diff
        return g0, wind(wx, to_west, to_east, fx), wind(wy, to_south, to_north, fy)

    @loop(0, ROWS // 8, unroll=2)
    def _(i, carry):
        x = pl.multiple_of(i * 8, 8)
        for z in range(2):
            sums = [acc[acc_at(q, z, x), :] for q in range(5)]
            made = chain(sums, *(coef[coef_at(name, z, x), :] for name in ("diff", "wx", "wy", "fx", "fy")))
            for f in range(3):
                grad[pl.ds((f * 2 + z) * ROWS + 8 + x, 8), :] = made[f]
        return carry

    for g in range(groups):
        members = range(g * SLOTS, min(blocks, (g + 1) * SLOTS))
        ks, valid, lasts, plume, _ = patches[g]
        seed = seeds[g]
        lam = [
            [[jnp.where(lasts == STEPS, seed[z][px][py], 0.0) for py in range(2)] for px in range(2)] for z in range(2)
        ]
        sums = [[zeros] * 5 for _ in range(2)]
        for t in range(STEPS - 1, 0, -1):
            state = plume[t]
            new = [[[None, None], [None, None]], [[None, None], [None, None]]]
            for z in range(2):
                k = ks[z]
                for px in range(2):
                    for py in range(2):
                        c, l = state[z][px][py], lam[z][px][py]
                        c_x, c_y = state[z][1 - px][py], state[z][px][1 - py]
                        l_x, l_y = lam[z][1 - px][py], lam[z][px][1 - py]
                        if px == 0:
                            to_east, to_west = c_x - c, c - pltpu.roll(c_x, 1, 0)
                            along_x = k["west"] * l_x + pltpu.roll(k["east"] * l_x, 1, 0)
                        else:
                            to_east, to_west = pltpu.roll(c_x, 7, 0) - c, c - c_x
                            along_x = pltpu.roll(k["west"] * l_x, 7, 0) + k["east"] * l_x
                        if py == 0:
                            to_north, to_south = c_y - c, c - pltpu.roll(c_y, 1, 1)
                            along_y = k["south"] * l_y + pltpu.roll(k["north"] * l_y, 1, 1)
                        else:
                            to_north, to_south = pltpu.roll(c_y, LANES - 1, 1) - c, c - c_y
                            along_y = pltpu.roll(k["south"] * l_y, LANES - 1, 1) + k["north"] * l_y
                        rise = state[1 - z][px][py] - 2.0 * c
                        for q, d in enumerate((to_east, to_west, to_north, to_south, rise)):
                            sums[z][q] = sums[z][q] + l * d
                        value = (k["centre"] * l + along_x) + (along_y + ks[1 - z]["diff"] * lam[1 - z][px][py])
                        new[z][px][py] = value + jnp.where(lasts == t, seed[z][px][py], 0.0)
            lam = new
        made = []
        for z in range(2):
            k = ks[z]
            made.append(chain(sums[z], k["diff"], k["wx"], k["wy"], k["fx"], k["fy"]))
        made = [[jnp.where(valid, made[z][f], 0.0) for z in range(2)] for f in range(3)]
        for r in members:
            here = slot == r % SLOTS
            x0, y0 = scalars[r, NSENS + 3], scalars[r, NSENS + 4]
            shift = (y0 - 8 * (r % SLOTS)) & (LANES - 1)
            for f in range(3):
                for z in range(2):
                    at = pl.ds((f * 2 + z) * ROWS + 8 + x0, 8)
                    grad[at, :] = grad[at, :] + pltpu.roll(jnp.where(here, made[f][z], 0.0), shift, 1)

    power = zeros
    for i in range(6 * ROWS // 8):
        g = grad[pl.ds(8 + i * 8, 8), :]
        power = power + g * g
    mean = jnp.sum(power, keepdims=True) * (1.0 / (6 * ROWS * LANES))
    scale = 1.0 / jnp.sqrt(mean + 1e-06)
    mine = me * rows + 8
    if rows % 8 == 0:
        mine = pl.multiple_of(mine, 8)
    direction_ref[...] = grad[pl.ds(mine, rows), :] * scale


def rounds(size):
    bits = [1 << i for i in range(size.bit_length() - 1)]
    return bits[2:] + bits[1::-1]


def solution(mesh):
    size = mesh.shape["rel"]
    bits = rounds(size)
    order = [0]
    for bit in bits:
        order = order + [at ^ bit for at in order]

    def local(coarse, background, sources, durations, counts, sensors, observed):
        rows = coarse.shape[0] // LANES
        block = -(-(rows + 2) // 8) * 8
        vmem = pl.BlockSpec(memory_space=pltpu.VMEM)
        smem = pl.BlockSpec(memory_space=pltpu.SMEM)
        packed = pl.pallas_call(
            pack_kernel,
            out_shape=jax.ShapeDtypeStruct((block, LANES), F32),
            in_specs=[vmem, vmem, vmem, smem, smem, smem],
            out_specs=vmem,
        )(coarse.reshape(rows, LANES), sensors, observed, sources, durations, counts)
        planes = pl.pallas_call(
            planes_kernel,
            out_shape=jax.ShapeDtypeStruct((FIELD, LANES), F32),
            in_specs=[vmem],
            out_specs=vmem,
            scratch_shapes=[pltpu.VMEM((4,) + background.shape[1:2] + (LANES,), F32)],
            compiler_params=pltpu.CompilerParams(vmem_limit_bytes=VMEM_LIMIT),
        )(background)
        held = packed
        for bit in bits:
            got = lax.ppermute(held, "rel", [(i, i ^ bit) for i in range(size)])
            if bit != bits[-1]:
                held = jnp.concatenate([held, got])
        direction, misfit = pl.pallas_call(
            functools.partial(gradient_kernel, order, rows),
            out_shape=(jax.ShapeDtypeStruct((rows, LANES), F32), jax.ShapeDtypeStruct((1,), F32)),
            in_specs=[vmem, vmem, vmem],
            out_specs=(vmem, smem),
            scratch_shapes=[
                pltpu.VMEM((6 * ROWS + 16, LANES), F32),
                pltpu.VMEM((14 * 2 * PLANE, LANES), F32),
                pltpu.VMEM((STEPS * FIELD, LANES), F32),
                pltpu.VMEM((FIELD, LANES), F32),
                pltpu.VMEM((FIELD, LANES), F32),
                pltpu.VMEM((10 * ROWS, LANES), F32),
                pltpu.VMEM((6 * ROWS + 16, LANES), F32),
                pltpu.VMEM((size, LANES), F32),
                pltpu.VMEM((size, LANES), F32),
                pltpu.VMEM((size, LANES), I32),
                pltpu.VMEM((size * NSENS, LANES), F32),
                pltpu.VMEM((size * NSENS, LANES), F32),
                pltpu.SMEM((size, LANES), I32),
                pltpu.SemaphoreType.DMA,
            ],
            compiler_params=pltpu.CompilerParams(vmem_limit_bytes=VMEM_LIMIT),
        )(held, got, planes)
        return direction.reshape(-1), misfit

    in_specs = (
        P(("grp", "rel")),
        P("grp", None, None),
        P(("grp", "rel")),
        P(("grp", "rel")),
        P(("grp", "rel")),
        P(("grp", "rel"), None),
        P(("grp", "rel"), None),
    )
    out_specs = (P(("grp", "rel")), P(("grp", "rel")))
    return jax.shard_map(local, mesh=mesh, in_specs=in_specs, out_specs=out_specs, check_vma=False)
```

```python
import functools

import jax
import jax.numpy as jnp
from jax import lax
from jax.experimental import pallas as pl
from jax.experimental.pallas import tpu as pltpu
from jax.sharding import PartitionSpec as P

STEPS = 6
NSENS = 64
PAD = 8
BATCH = 32
SLOTS = 16
ROWS = 128
LANES = 128
PLANE = ROWS + 2 * PAD
FIELD = 8 * PLANE
VMEM_LIMIT = 40 * 1024 * 1024
F32, BF16, I32 = jnp.float32, jnp.bfloat16, jnp.int32


def loop(first, end, unroll=None):
    def run(body):
        lax.fori_loop(first, end, body, None, unroll=unroll)

    return run


def plane_at(z, px, py):
    return ((z * 2 + px) * 2 + py) * PLANE + PAD


def split(value):
    high = value.astype(BF16)
    return high, (value - high.astype(F32)).astype(BF16)


def pack_kernel(source_ref, duration_ref, count_ref, coarse_ref, sensors_ref, observed_ref, out_ref, *rest):
    sensors, observed, sems = rest
    rows = coarse_ref.shape[0]
    pairs = ((coarse_ref, out_ref.at[pl.ds(0, rows), :]), (sensors_ref, sensors), (observed_ref, observed))
    copies = [pltpu.make_async_copy(src, dst, sems.at[i]) for i, (src, dst) in enumerate(pairs)]
    for copy in copies:
        copy.start()
    lane = lax.broadcasted_iota(I32, (1, LANES), 1)
    record = jnp.where(lane == 0, source_ref[0], jnp.where(lane == 1, duration_ref[0], count_ref[0]))
    record = jnp.where(lane == 3, lax.axis_index("rel"), record)
    for copy in copies:
        copy.wait()
    out_ref[pl.ds(rows, 1), pl.ds(0, NSENS)] = sensors[...].astype(F32)
    out_ref[pl.ds(rows, 1), pl.ds(NSENS, NSENS)] = observed[...]
    out_ref[pl.ds(rows + 1, 1), :] = record.astype(F32)
    spare = out_ref.shape[0] - rows - 2
    out_ref[pl.ds(rows + 2, spare), :] = jnp.zeros((spare, LANES), F32)


def planes_kernel(background_ref, out_ref, half_ref):
    width = background_ref.shape[2]
    out_ref[...] = jnp.zeros_like(out_ref)
    column = lax.broadcasted_iota(I32, (width, width), 1)
    row = lax.broadcasted_iota(I32, (width, width), 0)
    wanted = jnp.where(column < LANES, 2 * column, 2 * (column - LANES) + 1)
    pick = (row == wanted).astype(F32)
    for z in range(2):
        sorted_lanes = jnp.dot(
            background_ref[z], pick, precision=lax.Precision.HIGHEST, preferred_element_type=F32
        )
        for py in range(2):
            half_ref[z * 2 + py] = sorted_lanes[:, py * LANES : (py + 1) * LANES]
            for px in range(2):
                out_ref[pl.ds(plane_at(z, px, py), ROWS), :] = half_ref[z * 2 + py, pl.ds(px, ROWS, stride=2), :]


def gradient_kernel(
    order,
    rows,
    first_ref,
    second_ref,
    planes_ref,
    direction_ref,
    misfit_ref,
    par,
    coef,
    hist,
    lam_a,
    lam_b,
    acc,
    grad,
    sens_rows,
    meta_rows,
    table,
    gathered,
    scattered,
    scalars,
    sem,
):
    blocks = len(order)
    block = first_ref.shape[0] // (blocks // 2)
    me = lax.axis_index("rel")
    groups = -(-blocks // SLOTS)
    lane = lax.broadcasted_iota(I32, (8, LANES), 1)
    sub = lax.broadcasted_iota(I32, (8, LANES), 0)

    par[pl.ds(0, 8), :] = jnp.zeros((8, LANES), F32)
    par[pl.ds(8 + 6 * ROWS, 8), :] = jnp.zeros((8, LANES), F32)
    for p in range(blocks):
        ref = first_ref if p < blocks // 2 else second_ref
        at = (p % (blocks // 2)) * block
        owner = me ^ order[p]
        if rows % 8 == 0:
            place = pl.multiple_of(owner * rows + 8, 8)
        else:
            place = owner * rows + 8
        par[pl.ds(place, rows), :] = ref[pl.ds(at, rows), :]
        sens_rows[pl.ds(owner, 1), :] = ref[pl.ds(at + rows, 1), :]
        meta_rows[pl.ds(owner, 1), :] = ref[pl.ds(at + rows + 1, 1), :]

    half = blocks // 2
    wide = lax.broadcasted_iota(I32, (blocks, LANES), 1)
    place = lax.broadcasted_iota(I32, (blocks, LANES), 0)
    counts = jnp.broadcast_to(meta_rows[:, 2:3], (blocks, LANES))
    across = jnp.broadcast_to(counts.T[0:1, :], (blocks, blocks))
    down, left, top = counts[:, :blocks], wide[:, :blocks], place[:, :blocks]
    ahead = (down > across) | ((down == across) & (top < left))
    rank = jnp.sum(ahead.astype(F32), axis=0, keepdims=True)
    wanted = jnp.where(top < half, 2 * top, 2 * (top - half) + 1).astype(F32)
    order_by = (jnp.broadcast_to(rank, (blocks, blocks)) == wanted).astype(F32)
    at_least = jnp.sum((counts >= (wide - 8).astype(F32)).astype(F32), axis=0, keepdims=True)
    sorted_rows = jnp.dot(
        order_by,
        jnp.concatenate([sens_rows[...], meta_rows[...]], axis=1),
        precision=lax.Precision.HIGHEST,
        preferred_element_type=F32,
    )
    sorted_sens, meta = sorted_rows[:, :LANES], jnp.round(sorted_rows[:, LANES:]).astype(I32)

    pair_lane, pair_row = wide[:half], place[:half]
    first = pair_lane < NSENS

    def paired(value):
        return jnp.where(first, value[:half], value[half:])

    def spread(value):
        return jnp.broadcast_to(value, (blocks, LANES))

    turned = pltpu.roll(sorted_sens, NSENS, 1)
    sens = jnp.round(jnp.where(first, sorted_sens[:half], turned[half:])).astype(I32)
    watched = jnp.where(first, turned[:half], sorted_sens[half:])
    source, count, owner_of = spread(meta[:, 0:1]), spread(meta[:, 2:3]), spread(meta[:, 3:4])
    left_x = (((source >> 8) & 255) >> 1) - 3
    left_y = ((source & 255) >> 1) - 3
    fine_x, fine_y = (sens >> 8) & 255, sens & 255
    plane = (sens >> 16) * 4 + (fine_x & 1) * 2 + (fine_y & 1)
    cell_x, cell_y = fine_x >> 1, fine_y >> 1
    off_x, off_y = cell_x - paired(left_x), cell_y - paired(left_y)
    inside = (off_x >= 0) & (off_x < 8) & (off_y >= 0) & (off_y < 8)
    slot_of = (2 * pair_row + jnp.where(first, 0, 1)) % SLOTS
    patch_row = jnp.where(inside, plane * 8 + off_x, -1)
    patch_lane = jnp.where(inside, slot_of * 8 + off_y, -1)
    address = plane * PLANE + PAD + cell_x
    mine_of = paired(owner_of) == me
    for at, value in ((4, left_x), (5, left_y), (6, spread(meta[:, 0:1]))):
        meta = jnp.where(wide == at, value, meta)
    meta = jnp.where(wide >= 8, jnp.broadcast_to(at_least, (blocks, LANES)).astype(I32), meta)
    table[pl.ds(0, half), :] = address + (paired(count) - 1) * FIELD
    table[pl.ds(half, half), :] = address
    table[pl.ds(blocks, blocks), :] = meta
    copy = pltpu.make_async_copy(table, scalars, sem)
    copy.start()

    def about(j, lane_at):
        return scalars[blocks + (j % 2) * half + j // 2, lane_at]

    names = ("centre", "east", "west", "north", "south", "diff", "south0", "north1", "northr", "southl", "wx", "wy", "fx", "fy")
    index = {name: i for i, name in enumerate(names)}

    def coef_at(name, z, x):
        return pl.ds((index[name] * 2 + z) * PLANE + PAD + x, 8)

    zeros = jnp.zeros((8, LANES), F32)
    for z in range(2):
        coef[coef_at("east", z, -8), :] = zeros
        coef[coef_at("west", z, ROWS), :] = zeros

    def coefficients(p0, p1, p2):
        diff = 0.05 * jnp.exp(p0)
        t1, t2 = jnp.tanh(p1), jnp.tanh(p2)
        wx, wy = 0.08 * t1, 0.08 * t2
        east, west = diff - jnp.minimum(wx, 0.0), diff + jnp.maximum(wx, 0.0)
        north, south = diff - jnp.minimum(wy, 0.0), diff + jnp.maximum(wy, 0.0)
        centre = 1.0 - (east + west + north + south + 2.0 * diff)
        return dict(
            centre=centre, east=east, west=west, north=north, south=south, diff=diff,
            wx=wx, wy=wy, fx=0.08 * (1.0 - t1 * t1), fy=0.08 * (1.0 - t2 * t2),
        )

    @loop(0, ROWS // 8, unroll=4)
    def _(i, carry):
        x = pl.multiple_of(i * 8, 8)
        for z in range(2):
            p0, p1, p2 = (par[pl.ds((f * 2 + z) * ROWS + 8 + x, 8), :] for f in range(3))
            made = coefficients(p0, p1, p2)
            made["south0"] = jnp.where(lane == 0, 0.0, made["south"])
            made["north1"] = jnp.where(lane == LANES - 1, 0.0, made["north"])
            made["northr"] = jnp.where(lane == 0, 0.0, pltpu.roll(made["north"], 1, 1))
            made["southl"] = jnp.where(lane == LANES - 1, 0.0, pltpu.roll(made["south"], LANES - 1, 1))
            for name, value in made.items():
                coef[coef_at(name, z, x), :] = value
        return carry

    for p in range(8):
        for ref, fields in ((hist, STEPS), (lam_a, 1), (lam_b, 1)):
            for f in range(fields):
                ref[pl.ds(f * FIELD + p * PLANE, 8), :] = zeros
                ref[pl.ds(f * FIELD + p * PLANE + PAD + ROWS, 8), :] = zeros

    def load(ref, base, x):
        def at(z, px, py, shift=0):
            return ref[pl.ds(base + plane_at(z, px, py) + x + shift, 8), :]

        own = [[[at(z, px, py) for py in range(2)] for px in range(2)] for z in range(2)]
        odd = [[at(z, 1, py, -1) for py in range(2)] for z in range(2)]
        even = [[at(z, 0, py, 1) for py in range(2)] for z in range(2)]
        return own, odd, even

    def forward(src, src_base, dst, dst_base):
        @loop(0, ROWS // 8, unroll=16)
        def _(i, carry):
            x = pl.multiple_of(i * 8, 8)
            own, odd, even = load(src, src_base, x)
            for z in range(2):
                k = {
                    name: coef[coef_at(name, z, x), :]
                    for name in ("centre", "east", "west", "north", "south", "diff", "south0", "north1")
                }
                for px in range(2):
                    c0, c1 = own[z][px]
                    along_y = (
                        k["north"] * c1 + k["south0"] * pltpu.roll(c1, 1, 1),
                        k["north1"] * pltpu.roll(c0, LANES - 1, 1) + k["south"] * c0,
                    )
                    for py in range(2):
                        if px == 0:
                            along_x = k["east"] * own[z][1][py] + k["west"] * odd[z][py]
                        else:
                            along_x = k["east"] * even[z][py] + k["west"] * own[z][0][py]
                        new = (k["centre"] * own[z][px][py] + along_x) + (
                            along_y[py] + k["diff"] * own[1 - z][px][py]
                        )
                        dst[pl.ds(dst_base + plane_at(z, px, py) + x, 8), :] = new
            return carry

    forward(planes_ref, 0, hist, 0)
    for t in range(1, STEPS):
        forward(hist, (t - 1) * FIELD, hist, t * FIELD)

    copy.wait()

    @loop(0, half)
    def _(j, carry):
        to = pl.multiple_of(j * LANES, LANES)
        for s in range(LANES):
            gathered[pl.ds(to + s, 1), :] = hist[pl.ds(scalars[j, s], 1), :]
        return carry

    slot = lane >> 3
    patches = []
    for g in range(groups):
        members = range(g * SLOTS, min(blocks, (g + 1) * SLOTS))
        pp = [[zeros, zeros] for _ in range(3)]
        at_x, at_y, of_plane, lasts, emits = (jnp.zeros((8, LANES), I32) for _ in range(5))
        for r in members:
            here = slot == r % SLOTS
            src, dur, cnt, x0, y0 = (about(r, at) for at in (0, 1, 2, 4, 5))
            shift = (8 * (r % SLOTS) - y0) & (LANES - 1)
            for f in range(3):
                for z in range(2):
                    window = par[pl.ds((f * 2 + z) * ROWS + 8 + x0, 8), :]
                    pp[f][z] = jnp.where(here, pltpu.roll(window, shift, 1), pp[f][z])
            src_plane = (src >> 16) * 4 + ((src >> 8) & 1) * 2 + (src & 1)
            at_x = jnp.where(here, x0, at_x)
            at_y = jnp.where(here, y0, at_y)
            of_plane = jnp.where(here, src_plane, of_plane)
            emits = jnp.where(here, dur, emits)
            lasts = jnp.where(here, cnt, lasts)
        in_x, in_y = at_x + sub, at_y + (lane & 7)
        valid = (in_x >= 0) & (in_x < ROWS) & (in_y >= 0) & (in_y < LANES)
        ks = []
        for z in range(2):
            made = coefficients(pp[0][z], pp[1][z], pp[2][z])
            ks.append({name: jnp.where(valid, value, 0.0) for name, value in made.items()})
        spot = (sub == 3) & ((lane & 7) == 3)
        state = [[[zeros for _ in range(2)] for _ in range(2)] for _ in range(2)]
        plume = []
        for t in range(STEPS):
            plume.append(state)
            new = [[[None, None], [None, None]], [[None, None], [None, None]]]
            for z in range(2):
                k = ks[z]
                for px in range(2):
                    for py in range(2):
                        c = state[z][px][py]
                        other_x, other_y = state[z][1 - px][py], state[z][px][1 - py]
                        if px == 0:
                            along_x = k["east"] * other_x + k["west"] * pltpu.roll(other_x, 1, 0)
                        else:
                            along_x = k["east"] * pltpu.roll(other_x, 7, 0) + k["west"] * other_x
                        if py == 0:
                            along_y = k["north"] * other_y + k["south"] * pltpu.roll(other_y, 1, 1)
                        else:
                            along_y = k["north"] * pltpu.roll(other_y, LANES - 1, 1) + k["south"] * other_y
                        value = (k["centre"] * c + along_x) + (along_y + k["diff"] * state[1 - z][px][py])
                        emit = spot & (of_plane == z * 4 + px * 2 + py) & (t < emits)
                        value = value + jnp.where(emit, 4.0, 0.0)
                        new[z][px][py] = jnp.where(t < lasts, value, c)
            state = new
        patches.append((ks, valid, lasts, plume, state))

    def row_of(value, j):
        return jnp.broadcast_to(value[j : j + 1, :], (LANES, LANES))

    def with_rows(a, b):
        return lax.dot_general(a, b, (((1,), (1,)), ((), ())), preferred_element_type=F32)

    sub_sq = lax.broadcasted_iota(I32, (LANES, LANES), 0)
    lane_sq = lax.broadcasted_iota(I32, (LANES, LANES), 1)
    diagonal = sub_sq == lane_sq
    batch = (lane_sq // BATCH) == (sub_sq // BATCH)
    row_id = address.astype(F32)
    row_down = row_id.T
    loss = jnp.zeros((1, LANES), F32)
    seeds = []
    for g in range(groups):
        final = patches[g][4]
        flat = jnp.concatenate([final[z][px][py] for z in range(2) for px in range(2) for py in range(2)], axis=0)
        flat = jnp.concatenate(split(flat), axis=0)
        seed = jnp.zeros((LANES, LANES), F32)
        for j in range(g * SLOTS // 2, min(half, (g + 1) * SLOTS // 2)):
            at_lane = (sub_sq == row_of(cell_y, j)).astype(F32).astype(BF16)
            at_patch = (sub_sq == row_of(patch_lane, j)).astype(F32).astype(BF16)
            put = sub_sq[:NSENS] == row_of(patch_row, j)[:NSENS]
            high, low = split(gathered[pl.ds(j * LANES, LANES), :])
            far = jnp.dot(high, at_lane, preferred_element_type=F32) + jnp.dot(low, at_lane, preferred_element_type=F32)
            far = jnp.sum(jnp.where(diagonal, far, 0.0), axis=0, keepdims=True)
            near = jnp.dot(flat, at_patch, preferred_element_type=F32)
            near = jnp.sum(jnp.where(put, near[:NSENS] + near[NSENS:], 0.0), axis=0, keepdims=True)
            residual = far + near - watched[j : j + 1, :]
            loss = loss + jnp.where(mine_of[j : j + 1, :], residual * residual, 0.0)
            same = (jnp.broadcast_to(row_down[:, j : j + 1], (LANES, LANES)) == row_of(row_id, j)) & batch
            high, low = split(jnp.where(same, jnp.broadcast_to(residual, (LANES, LANES)), 0.0))
            scattered[pl.ds(j * LANES, LANES), :] = with_rows(high, at_lane) + with_rows(low, at_lane)
            put = jnp.where(put, jnp.broadcast_to(residual, (NSENS, LANES)), 0.0)
            seed = seed + with_rows(jnp.concatenate(split(put), axis=0), at_patch)
        seed = seed[:NSENS] + seed[NSENS:]
        seeds.append(
            [[[seed[((z * 2 + px) * 2 + py) * 8 :][:8] for py in range(2)] for px in range(2)] for z in range(2)]
        )
    misfit_ref[0] = jnp.sum(loss) * (0.5 / NSENS)

    def seed_sensors(ref, t):
        @loop(scalars[blocks, 8 + t + 1], scalars[blocks, 8 + t])
        def _(j, carry):
            row, column = j // 2, (j % 2) * NSENS
            at = pl.multiple_of(j * NSENS, NSENS)
            for part in range(0, NSENS, BATCH):
                spots = [pl.ds(scalars[half + row, column + s], 1) for s in range(part, part + BATCH)]
                news = [ref[spot, :] + scattered[pl.ds(at + part + s, 1), :] for s, spot in enumerate(spots)]
                for spot, new in zip(spots, news):
                    ref[spot, :] = new
            return carry

    def acc_at(q, z, x):
        return pl.ds((q * 2 + z) * ROWS + x, 8)

    def backward(src, dst, conc, conc_base, first, last):
        @loop(0, ROWS // 8, unroll=16)
        def _(i, carry):
            x = pl.multiple_of(i * 8, 8)
            lam, lam_odd, lam_even = load(src, 0, x)
            own, odd, even = load(conc, conc_base, x)
            diffs = [coef[coef_at("diff", z, x), :] for z in range(2)]
            for z in range(2):
                if not last:
                    k = {
                        name: coef[coef_at(name, z, x), :]
                        for name in ("centre", "east", "west", "north", "south", "northr", "southl")
                    }
                    east_m, west_p = coef[coef_at("east", z, x - 1), :], coef[coef_at("west", z, x + 1), :]
                    for px in range(2):
                        l0, l1 = lam[z][px]
                        along_y = (
                            k["south"] * l1 + k["northr"] * pltpu.roll(l1, 1, 1),
                            k["southl"] * pltpu.roll(l0, LANES - 1, 1) + k["north"] * l0,
                        )
                        for py in range(2):
                            if px == 0:
                                along_x = k["west"] * lam[z][1][py] + east_m * lam_odd[z][py]
                            else:
                                along_x = west_p * lam_even[z][py] + k["east"] * lam[z][0][py]
                            new = (k["centre"] * lam[z][px][py] + along_x) + (
                                along_y[py] + diffs[1 - z] * lam[1 - z][px][py]
                            )
                            dst[pl.ds(plane_at(z, px, py) + x, 8), :] = new
                sums = [None] * 5
                for px in range(2):
                    c0, c1 = own[z][px]
                    mid = c1 - c0
                    to_north = (mid, jnp.where(lane == LANES - 1, 0.0, pltpu.roll(c0, LANES - 1, 1)) - c1)
                    to_south = (c0 - jnp.where(lane == 0, 0.0, pltpu.roll(c1, 1, 1)), mid)
                    for py in range(2):
                        c, l = own[z][px][py], lam[z][px][py]
                        mid_x = own[z][1][py] - own[z][0][py]
                        if px == 0:
                            to_east, to_west = mid_x, c - odd[z][py]
                        else:
                            to_east, to_west = even[z][py] - c, mid_x
                        rise = own[1 - z][px][py] - 2.0 * c
                        for q, d in enumerate((to_east, to_west, to_north[py], to_south[py], rise)):
                            term = l * d
                            sums[q] = term if sums[q] is None else sums[q] + term
                for q in range(5):
                    at = acc_at(q, z, x)
                    acc[at, :] = sums[q] if first else acc[at, :] + sums[q]
            return carry

    @loop(0, FIELD // 64)
    def _(i, carry):
        lam_a[pl.ds(pl.multiple_of(i * 64, 64), 64), :] = jnp.zeros((64, LANES), F32)
        return carry

    src, dst = lam_a, lam_b
    for t in range(STEPS - 1, -1, -1):
        seed_sensors(src, t + 1)
        if t == 0:
            backward(src, dst, planes_ref, 0, False, True)
        else:
            backward(src, dst, hist, (t - 1) * FIELD, t == STEPS - 1, False)
        src, dst = dst, src

    def chain(sums, diff, wx, wy, fx, fy):
        to_east, to_west, to_north, to_south, rise = sums

        def wind(w, up, down, factor):
            plus = jnp.where(w > 0.0, 1.0, jnp.where(w == 0.0, 0.5, 0.0))
            return -(plus * up + (1.0 - plus) * down) * factor

        g0 = (to_east - to_west + to_north - to_south + rise) * diff
        return g0, wind(wx, to_west, to_east, fx), wind(wy, to_south, to_north, fy)

    @loop(0, ROWS // 8, unroll=16)
    def _(i, carry):
        x = pl.multiple_of(i * 8, 8)
        for z in range(2):
            sums = [acc[acc_at(q, z, x), :] for q in range(5)]
            made = chain(sums, *(coef[coef_at(name, z, x), :] for name in ("diff", "wx", "wy", "fx", "fy")))
            for f in range(3):
                grad[pl.ds((f * 2 + z) * ROWS + 8 + x, 8), :] = made[f]
        return carry

    for g in range(groups):
        members = range(g * SLOTS, min(blocks, (g + 1) * SLOTS))
        ks, valid, lasts, plume, _ = patches[g]
        seed = seeds[g]
        lam = [
            [[jnp.where(lasts == STEPS, seed[z][px][py], 0.0) for py in range(2)] for px in range(2)] for z in range(2)
        ]
        sums = [[zeros] * 5 for _ in range(2)]
        for t in range(STEPS - 1, 0, -1):
            state = plume[t]
            new = [[[None, None], [None, None]], [[None, None], [None, None]]]
            for z in range(2):
                k = ks[z]
                for px in range(2):
                    for py in range(2):
                        c, l = state[z][px][py], lam[z][px][py]
                        c_x, c_y = state[z][1 - px][py], state[z][px][1 - py]
                        l_x, l_y = lam[z][1 - px][py], lam[z][px][1 - py]
                        if px == 0:
                            to_east, to_west = c_x - c, c - pltpu.roll(c_x, 1, 0)
                            along_x = k["west"] * l_x + pltpu.roll(k["east"] * l_x, 1, 0)
                        else:
                            to_east, to_west = pltpu.roll(c_x, 7, 0) - c, c - c_x
                            along_x = pltpu.roll(k["west"] * l_x, 7, 0) + k["east"] * l_x
                        if py == 0:
                            to_north, to_south = c_y - c, c - pltpu.roll(c_y, 1, 1)
                            along_y = k["south"] * l_y + pltpu.roll(k["north"] * l_y, 1, 1)
                        else:
                            to_north, to_south = pltpu.roll(c_y, LANES - 1, 1) - c, c - c_y
                            along_y = pltpu.roll(k["south"] * l_y, LANES - 1, 1) + k["north"] * l_y
                        rise = state[1 - z][px][py] - 2.0 * c
                        for q, d in enumerate((to_east, to_west, to_north, to_south, rise)):
                            sums[z][q] = sums[z][q] + l * d
                        value = (k["centre"] * l + along_x) + (along_y + ks[1 - z]["diff"] * lam[1 - z][px][py])
                        new[z][px][py] = value + jnp.where(lasts == t, seed[z][px][py], 0.0)
            lam = new
        made = []
        for z in range(2):
            k = ks[z]
            made.append(chain(sums[z], k["diff"], k["wx"], k["wy"], k["fx"], k["fy"]))
        made = [[jnp.where(valid, made[z][f], 0.0) for z in range(2)] for f in range(3)]
        for r in members:
            here = slot == r % SLOTS
            x0, y0 = about(r, 4), about(r, 5)
            shift = (y0 - 8 * (r % SLOTS)) & (LANES - 1)
            spots = [pl.ds((f * 2 + z) * ROWS + 8 + x0, 8) for f in range(3) for z in range(2)]
            news = [
                grad[spots[f * 2 + z], :] + pltpu.roll(jnp.where(here, made[f][z], 0.0), shift, 1)
                for f in range(3)
                for z in range(2)
            ]
            for spot, new in zip(spots, news):
                grad[spot, :] = new

    power = zeros
    for i in range(6 * ROWS // 8):
        g = grad[pl.ds(8 + i * 8, 8), :]
        power = power + g * g
    mean = jnp.sum(power, keepdims=True) * (1.0 / (6 * ROWS * LANES))
    scale = 1.0 / jnp.sqrt(mean + 1e-06)
    mine = me * rows + 8
    if rows % 8 == 0:
        mine = pl.multiple_of(mine, 8)
    direction_ref[...] = grad[pl.ds(mine, rows), :] * scale


def rounds(size):
    bits = [1 << i for i in range(size.bit_length() - 1)]
    return bits[2:] + bits[1::-1]


def solution(mesh):
    size = mesh.shape["rel"]
    bits = rounds(size)
    order = [0]
    for bit in bits:
        order = order + [at ^ bit for at in order]

    def local(coarse, background, sources, durations, counts, sensors, observed):
        rows = coarse.shape[0] // LANES
        block = -(-(rows + 2) // 8) * 8
        vmem = pl.BlockSpec(memory_space=pltpu.VMEM)
        smem = pl.BlockSpec(memory_space=pltpu.SMEM)
        packed = pl.pallas_call(
            pack_kernel,
            out_shape=pltpu.VMEM((block, LANES), F32),
            in_specs=[smem] * 3 + [pl.BlockSpec(memory_space=pl.ANY)] * 3,
            out_specs=vmem,
            scratch_shapes=[
                pltpu.VMEM((1, NSENS), I32),
                pltpu.VMEM((1, NSENS), F32),
                pltpu.SemaphoreType.DMA((3,)),
            ],
        )(sources, durations, counts, coarse.reshape(rows, LANES), sensors, observed)
        planes = pl.pallas_call(
            planes_kernel,
            out_shape=jax.ShapeDtypeStruct((FIELD, LANES), F32),
            in_specs=[vmem],
            out_specs=vmem,
            scratch_shapes=[pltpu.VMEM((4,) + background.shape[1:2] + (LANES,), F32)],
            compiler_params=pltpu.CompilerParams(vmem_limit_bytes=VMEM_LIMIT),
        )(background)
        held = packed.reshape(-1)
        for bit in bits:
            got = lax.ppermute(held, "rel", [(i, i ^ bit) for i in range(size)])
            if bit != bits[-1]:
                own = lax.optimization_barrier(jnp.concatenate([held, jnp.zeros_like(held)]))
                held = lax.optimization_barrier(lax.dynamic_update_slice(own, got, (held.shape[0],)))
        direction, misfit = pl.pallas_call(
            functools.partial(gradient_kernel, order, rows),
            out_shape=(jax.ShapeDtypeStruct((rows, LANES), F32), jax.ShapeDtypeStruct((1,), F32)),
            in_specs=[vmem, vmem, vmem],
            out_specs=(vmem, smem),
            scratch_shapes=[
                pltpu.VMEM((6 * ROWS + 16, LANES), F32),
                pltpu.VMEM((14 * 2 * PLANE, LANES), F32),
                pltpu.VMEM((STEPS * FIELD, LANES), F32),
                pltpu.VMEM((FIELD, LANES), F32),
                pltpu.VMEM((FIELD, LANES), F32),
                pltpu.VMEM((10 * ROWS, LANES), F32),
                pltpu.VMEM((6 * ROWS + 16, LANES), F32),
                pltpu.VMEM((size, LANES), F32),
                pltpu.VMEM((size, LANES), F32),
                pltpu.VMEM((2 * size, LANES), I32),
                pltpu.VMEM((size * NSENS, LANES), F32),
                pltpu.VMEM((size * NSENS, LANES), F32),
                pltpu.SMEM((2 * size, LANES), I32),
                pltpu.SemaphoreType.DMA,
            ],
            compiler_params=pltpu.CompilerParams(vmem_limit_bytes=VMEM_LIMIT),
        )(held.reshape(-1, LANES), got.reshape(-1, LANES), planes)
        return direction.reshape(-1), misfit

    in_specs = (
        P(("grp", "rel")),
        P("grp", None, None),
        P(("grp", "rel")),
        P(("grp", "rel")),
        P(("grp", "rel")),
        P(("grp", "rel"), None),
        P(("grp", "rel"), None),
    )
    out_specs = (P(("grp", "rel")), P(("grp", "rel")))
    return jax.shard_map(local, mesh=mesh, in_specs=in_specs, out_specs=out_specs, check_vma=False)
```

```python
import functools

import jax
import jax.numpy as jnp
from jax import lax
from jax.experimental import pallas as pl
from jax.experimental.pallas import tpu as pltpu
from jax.sharding import PartitionSpec as P

STEPS = 6
NSENS = 64
PAD = 8
BATCH = 32
SLOTS = 16
PAIRS = SLOTS // 2
ROWS = 128
LANES = 128
PLANE = ROWS + 2 * PAD
FIELD = 8 * PLANE
VMEM_LIMIT = 40 * 1024 * 1024
F32, BF16, I32 = jnp.float32, jnp.bfloat16, jnp.int32


def loop(first, end, unroll=None):
    def run(body):
        lax.fori_loop(first, end, body, None, unroll=unroll)

    return run


def plane_at(z, px, py):
    return ((z * 2 + px) * 2 + py) * PLANE + PAD


def split(value):
    high = value.astype(BF16)
    return high, (value - high.astype(F32)).astype(BF16)


def pack_kernel(source_ref, duration_ref, count_ref, coarse_ref, sensors_ref, observed_ref, out_ref, *rest):
    sensors, observed, sems = rest
    rows = coarse_ref.shape[0]
    pairs = ((coarse_ref, out_ref.at[pl.ds(0, rows), :]), (sensors_ref, sensors), (observed_ref, observed))
    copies = [pltpu.make_async_copy(src, dst, sems.at[i]) for i, (src, dst) in enumerate(pairs)]
    for copy in copies:
        copy.start()
    lane = lax.broadcasted_iota(I32, (1, LANES), 1)
    record = jnp.where(lane == 0, source_ref[0], jnp.where(lane == 1, duration_ref[0], count_ref[0]))
    for copy in copies:
        copy.wait()
    out_ref[pl.ds(rows, 1), pl.ds(0, NSENS)] = sensors[...].astype(F32)
    out_ref[pl.ds(rows, 1), pl.ds(NSENS, NSENS)] = observed[...]
    out_ref[pl.ds(rows + 1, 1), :] = record.astype(F32)
    spare = out_ref.shape[0] - rows - 2
    out_ref[pl.ds(rows + 2, spare), :] = jnp.zeros((spare, LANES), F32)


def planes_kernel(background_ref, out_ref, half_ref):
    width = background_ref.shape[2]
    out_ref[...] = jnp.zeros_like(out_ref)
    column = lax.broadcasted_iota(I32, (width, width), 1)
    row = lax.broadcasted_iota(I32, (width, width), 0)
    wanted = jnp.where(column < LANES, 2 * column, 2 * (column - LANES) + 1)
    pick = (row == wanted).astype(F32)
    for z in range(2):
        sorted_lanes = jnp.dot(
            background_ref[z], pick, precision=lax.Precision.HIGHEST, preferred_element_type=F32
        )
        for py in range(2):
            half_ref[z * 2 + py] = sorted_lanes[:, py * LANES : (py + 1) * LANES]
            for px in range(2):
                out_ref[pl.ds(plane_at(z, px, py), ROWS), :] = half_ref[z * 2 + py, pl.ds(px, ROWS, stride=2), :]


def gradient_kernel(
    order,
    rows,
    first_ref,
    second_ref,
    planes_ref,
    direction_ref,
    misfit_ref,
    par,
    coef,
    hist,
    lam_a,
    lam_b,
    acc,
    grad,
    sens_rows,
    meta_rows,
    table,
    gathered,
    scattered,
    seed_rows,
    sensor_ints,
    sensor_reals,
    flats,
    patch_seeds,
    scalars,
    sem,
):
    blocks = len(order)
    block = first_ref.shape[0] // (blocks // 2)
    me = lax.axis_index("rel")
    half = blocks // 2
    groups = -(-half // PAIRS)
    lane = lax.broadcasted_iota(I32, (8, LANES), 1)
    sub = lax.broadcasted_iota(I32, (8, LANES), 0)

    par[pl.ds(0, 8), :] = jnp.zeros((8, LANES), F32)
    par[pl.ds(8 + 6 * ROWS, 8), :] = jnp.zeros((8, LANES), F32)
    for p in range(blocks):
        ref = first_ref if p < blocks // 2 else second_ref
        at = (p % (blocks // 2)) * block
        owner = me ^ order[p]
        if rows % 8 == 0:
            place = pl.multiple_of(owner * rows + 8, 8)
        else:
            place = owner * rows + 8
        par[pl.ds(place, rows), :] = ref[pl.ds(at, rows), :]
        stand = (owner // SLOTS) * PAIRS + owner % PAIRS + ((owner // PAIRS) % 2) * half
        sens_rows[pl.ds(stand, 1), :] = ref[pl.ds(at + rows, 1), :]
        meta_rows[pl.ds(stand, 1), :] = ref[pl.ds(at + rows + 1, 1), :]

    wide = lax.broadcasted_iota(I32, (blocks, LANES), 1)
    place = lax.broadcasted_iota(I32, (blocks, LANES), 0)
    meta = meta_rows[...].astype(I32)

    pair_lane, pair_row = wide[:half], place[:half]
    first = pair_lane < NSENS

    def paired(value):
        return jnp.where(first, value[:half], value[half:])

    def spread(value):
        return jnp.broadcast_to(value, (blocks, LANES))

    straight = sens_rows[...]
    turned = pltpu.roll(straight, NSENS, 1)
    sens = jnp.where(first, straight[:half], turned[half:]).astype(I32)
    watched = jnp.where(first, turned[:half], straight[half:])
    source, count = spread(meta[:, 0:1]), spread(meta[:, 2:3])
    left_x = (((source >> 8) & 255) >> 1) - 3
    left_y = ((source & 255) >> 1) - 3
    fine_x, fine_y = (sens >> 8) & 255, sens & 255
    plane = (sens >> 16) * 4 + (fine_x & 1) * 2 + (fine_y & 1)
    cell_x, cell_y = fine_x >> 1, fine_y >> 1
    off_x, off_y = cell_x - paired(left_x), cell_y - paired(left_y)
    inside = (off_x >= 0) & (off_x < 8) & (off_y >= 0) & (off_y < 8)
    slot_of = pair_row % PAIRS + jnp.where(first, 0, PAIRS)
    patch_row = jnp.where(inside, plane * 8 + off_x, -1)
    patch_lane = jnp.where(inside, slot_of * 8 + off_y, -1)
    address = plane * PLANE + PAD + cell_x
    for at, value in ((4, left_x), (5, left_y)):
        meta = jnp.where(wide == at, value, meta)
    table[pl.ds(0, half), :] = address + (paired(count) - 1) * FIELD
    table[pl.ds(half, blocks), :] = meta
    copy = pltpu.make_async_copy(table, scalars, sem)
    copy.start()
    sensor_reals[pl.ds(0, half), :] = watched
    sensor_reals[pl.ds(half, half), :] = ((pair_row // PAIRS) * SLOTS + slot_of == me).astype(F32)
    for i, value in enumerate((cell_y, patch_lane, patch_row, address)):
        sensor_ints[pl.ds(i * half, half), :] = value

    def about(j, lane_at):
        return scalars[half + (j // SLOTS) * PAIRS + j % PAIRS + (j // PAIRS % 2) * half, lane_at]

    names = ("centre", "east", "west", "north", "south", "diff", "south0", "north1", "northr", "southl", "wx", "wy", "fx", "fy")
    index = {name: i for i, name in enumerate(names)}

    def coef_at(name, z, x):
        return pl.ds((index[name] * 2 + z) * PLANE + PAD + x, 8)

    zeros = jnp.zeros((8, LANES), F32)
    for z in range(2):
        coef[coef_at("east", z, -8), :] = zeros
        coef[coef_at("west", z, ROWS), :] = zeros

    def coefficients(p0, p1, p2):
        diff = 0.05 * jnp.exp(p0)
        t1, t2 = jnp.tanh(p1), jnp.tanh(p2)
        wx, wy = 0.08 * t1, 0.08 * t2
        east, west = diff - jnp.minimum(wx, 0.0), diff + jnp.maximum(wx, 0.0)
        north, south = diff - jnp.minimum(wy, 0.0), diff + jnp.maximum(wy, 0.0)
        centre = 1.0 - (east + west + north + south + 2.0 * diff)
        return dict(
            centre=centre, east=east, west=west, north=north, south=south, diff=diff,
            wx=wx, wy=wy, fx=0.08 * (1.0 - t1 * t1), fy=0.08 * (1.0 - t2 * t2),
        )

    @loop(0, ROWS // 8, unroll=16)
    def _(i, carry):
        x = pl.multiple_of(i * 8, 8)
        for z in range(2):
            p0, p1, p2 = (par[pl.ds((f * 2 + z) * ROWS + 8 + x, 8), :] for f in range(3))
            made = coefficients(p0, p1, p2)
            made["south0"] = jnp.where(lane == 0, 0.0, made["south"])
            made["north1"] = jnp.where(lane == LANES - 1, 0.0, made["north"])
            made["northr"] = jnp.where(lane == 0, 0.0, pltpu.roll(made["north"], 1, 1))
            made["southl"] = jnp.where(lane == LANES - 1, 0.0, pltpu.roll(made["south"], LANES - 1, 1))
            for name, value in made.items():
                coef[coef_at(name, z, x), :] = value
        return carry

    for p in range(8):
        for ref, fields in ((hist, STEPS), (seed_rows, STEPS), (lam_a, 1), (lam_b, 1)):
            for f in range(fields):
                ref[pl.ds(f * FIELD + p * PLANE, 8), :] = zeros
                ref[pl.ds(f * FIELD + p * PLANE + PAD + ROWS, 8), :] = zeros

    def load(ref, base, x):
        def at(z, px, py, shift=0):
            return ref[pl.ds(base + plane_at(z, px, py) + x + shift, 8), :]

        own = [[[at(z, px, py) for py in range(2)] for px in range(2)] for z in range(2)]
        odd = [[at(z, 1, py, -1) for py in range(2)] for z in range(2)]
        even = [[at(z, 0, py, 1) for py in range(2)] for z in range(2)]
        return own, odd, even

    def forward(src, src_base, dst, dst_base):
        @loop(0, ROWS // 8, unroll=16)
        def _(i, carry):
            x = pl.multiple_of(i * 8, 8)
            own, odd, even = load(src, src_base, x)
            for z in range(2):
                k = {
                    name: coef[coef_at(name, z, x), :]
                    for name in ("centre", "east", "west", "north", "south", "diff", "south0", "north1")
                }
                for px in range(2):
                    c0, c1 = own[z][px]
                    along_y = (
                        k["north"] * c1 + k["south0"] * pltpu.roll(c1, 1, 1),
                        k["north1"] * pltpu.roll(c0, LANES - 1, 1) + k["south"] * c0,
                    )
                    for py in range(2):
                        if px == 0:
                            along_x = k["east"] * own[z][1][py] + k["west"] * odd[z][py]
                        else:
                            along_x = k["east"] * even[z][py] + k["west"] * own[z][0][py]
                        new = (k["centre"] * own[z][px][py] + along_x) + (
                            along_y[py] + k["diff"] * own[1 - z][px][py]
                        )
                        dst[pl.ds(dst_base + plane_at(z, px, py) + x, 8), :] = new
                        seed_rows[pl.ds(dst_base + plane_at(z, px, py) + x, 8), :] = zeros
            return carry

    copy.wait()

    slot = lane >> 3
    patches = []
    for g in range(groups):
        members = range(g * SLOTS, min(blocks, (g + 1) * SLOTS))
        pp = [[zeros, zeros] for _ in range(3)]
        at_x, at_y, of_plane, lasts, emits = (jnp.zeros((8, LANES), I32) for _ in range(5))
        for r in members:
            here = slot == r % SLOTS
            src, dur, cnt, x0, y0 = (about(r, at) for at in (0, 1, 2, 4, 5))
            shift = (8 * (r % SLOTS) - y0) & (LANES - 1)
            for f in range(3):
                for z in range(2):
                    window = par[pl.ds((f * 2 + z) * ROWS + 8 + x0, 8), :]
                    pp[f][z] = jnp.where(here, pltpu.roll(window, shift, 1), pp[f][z])
            src_plane = (src >> 16) * 4 + ((src >> 8) & 1) * 2 + (src & 1)
            at_x = jnp.where(here, x0, at_x)
            at_y = jnp.where(here, y0, at_y)
            of_plane = jnp.where(here, src_plane, of_plane)
            emits = jnp.where(here, dur, emits)
            lasts = jnp.where(here, cnt, lasts)
        in_x, in_y = at_x + sub, at_y + (lane & 7)
        valid = (in_x >= 0) & (in_x < ROWS) & (in_y >= 0) & (in_y < LANES)
        ks = []
        for z in range(2):
            made = coefficients(pp[0][z], pp[1][z], pp[2][z])
            ks.append({name: jnp.where(valid, value, 0.0) for name, value in made.items()})
        spot = (sub == 3) & ((lane & 7) == 3)
        state = [[[zeros for _ in range(2)] for _ in range(2)] for _ in range(2)]
        patches.append((ks, valid, lasts, of_plane, emits, spot, [state]))

    def plume_forward(t):
        for ks, _, lasts, of_plane, emits, spot, plume in patches:
            state = plume[t]
            new = [[[None, None], [None, None]], [[None, None], [None, None]]]
            for z in range(2):
                k = ks[z]
                for px in range(2):
                    for py in range(2):
                        c = state[z][px][py]
                        other_x, other_y = state[z][1 - px][py], state[z][px][1 - py]
                        if px == 0:
                            along_x = k["east"] * other_x + k["west"] * pltpu.roll(other_x, 1, 0)
                        else:
                            along_x = k["east"] * pltpu.roll(other_x, 7, 0) + k["west"] * other_x
                        if py == 0:
                            along_y = k["north"] * other_y + k["south"] * pltpu.roll(other_y, 1, 1)
                        else:
                            along_y = k["north"] * pltpu.roll(other_y, LANES - 1, 1) + k["south"] * other_y
                        value = (k["centre"] * c + along_x) + (along_y + k["diff"] * state[1 - z][px][py])
                        emit = spot & (of_plane == z * 4 + px * 2 + py) & (t < emits)
                        value = value + jnp.where(emit, 4.0, 0.0)
                        new[z][px][py] = jnp.where(t < lasts, value, c)
            plume.append(new)

    for t in range(STEPS):
        plume_forward(t)
        if t == 0:
            forward(planes_ref, 0, hist, 0)
        else:
            forward(hist, (t - 1) * FIELD, hist, t * FIELD)

    def with_rows(a, b):
        return lax.dot_general(a, b, (((1,), (1,)), ((), ())), preferred_element_type=F32)

    sub_sq = lax.broadcasted_iota(I32, (LANES, LANES), 0)
    lane_sq = lax.broadcasted_iota(I32, (LANES, LANES), 1)
    diagonal = sub_sq == lane_sq
    batch = (lane_sq // BATCH) == (sub_sq // BATCH)
    for g in range(groups):
        final = patches[g][-1][STEPS]
        flat = jnp.concatenate([final[z][px][py] for z in range(2) for px in range(2) for py in range(2)], axis=0)
        flats[pl.ds(g * LANES, LANES), :] = jnp.concatenate(split(flat), axis=0)
        patch_seeds[pl.ds(g * LANES, LANES), :] = jnp.zeros((LANES, LANES), F32)
    misfit_row = sensor_reals.at[pl.ds(2 * half, 1), :]
    misfit_row[...] = jnp.zeros((1, LANES), F32)

    @loop(0, half, unroll=PAIRS)
    def _(j, carry):
        to = pl.multiple_of(j * LANES, LANES)
        group = pl.ds(pl.multiple_of(j // PAIRS * LANES, LANES), LANES)
        for s in range(LANES):
            gathered[pl.ds(to + s, 1), :] = hist[pl.ds(scalars[j, s], 1), :]

        def row_of(i):
            return jnp.broadcast_to(sensor_ints[pl.ds(i * half + j, 1), :], (LANES, LANES))

        at_lane = (sub_sq == row_of(0)).astype(F32).astype(BF16)
        at_patch = (sub_sq == row_of(1)).astype(F32).astype(BF16)
        put = sub_sq[:NSENS] == row_of(2)[:NSENS]
        high, low = split(gathered[pl.ds(to, LANES), :])
        far = jnp.dot(high, at_lane, preferred_element_type=F32) + jnp.dot(low, at_lane, preferred_element_type=F32)
        far = jnp.sum(jnp.where(diagonal, far, 0.0), axis=0, keepdims=True)
        near = jnp.dot(flats[group, :], at_patch, preferred_element_type=F32)
        near = jnp.sum(jnp.where(put, near[:NSENS] + near[NSENS:], 0.0), axis=0, keepdims=True)
        residual = far + near - sensor_reals[pl.ds(j, 1), :]
        misfit_row[...] += sensor_reals[pl.ds(half + j, 1), :] * residual * residual
        row_id = row_of(3).astype(F32)
        same = (row_id == row_id.T) & batch
        high, low = split(jnp.where(same, jnp.broadcast_to(residual, (LANES, LANES)), 0.0))
        scattered[pl.ds(to, LANES), :] = with_rows(high, at_lane) + with_rows(low, at_lane)
        put = jnp.where(put, jnp.broadcast_to(residual, (NSENS, LANES)), 0.0)
        patch_seeds[group, :] += with_rows(jnp.concatenate(split(put), axis=0), at_patch)
        for part in range(0, LANES, BATCH):
            spots = [pl.ds(scalars[j, s], 1) for s in range(part, part + BATCH)]
            news = [seed_rows[spot, :] + scattered[pl.ds(to + part + s, 1), :] for s, spot in enumerate(spots)]
            for spot, new in zip(spots, news):
                seed_rows[spot, :] = new

    seeds = []
    for g in range(groups):
        seed = patch_seeds[pl.ds(g * LANES, NSENS), :] + patch_seeds[pl.ds(g * LANES + NSENS, NSENS), :]
        seeds.append(
            [[[seed[((z * 2 + px) * 2 + py) * 8 :][:8] for py in range(2)] for px in range(2)] for z in range(2)]
        )
    misfit_ref[0] = jnp.sum(misfit_row[...]) * (0.5 / NSENS)

    def acc_at(q, z, x):
        return pl.ds((q * 2 + z) * ROWS + x, 8)

    def backward(src, src_base, dst, seed_base, conc, conc_base, first, last):
        @loop(0, ROWS // 8, unroll=16)
        def _(i, carry):
            x = pl.multiple_of(i * 8, 8)
            lam, lam_odd, lam_even = load(src, src_base, x)
            own, odd, even = load(conc, conc_base, x)
            diffs = [coef[coef_at("diff", z, x), :] for z in range(2)]
            for z in range(2):
                if not last:
                    k = {
                        name: coef[coef_at(name, z, x), :]
                        for name in ("centre", "east", "west", "north", "south", "northr", "southl")
                    }
                    east_m, west_p = coef[coef_at("east", z, x - 1), :], coef[coef_at("west", z, x + 1), :]
                    for px in range(2):
                        l0, l1 = lam[z][px]
                        along_y = (
                            k["south"] * l1 + k["northr"] * pltpu.roll(l1, 1, 1),
                            k["southl"] * pltpu.roll(l0, LANES - 1, 1) + k["north"] * l0,
                        )
                        for py in range(2):
                            if px == 0:
                                along_x = k["west"] * lam[z][1][py] + east_m * lam_odd[z][py]
                            else:
                                along_x = west_p * lam_even[z][py] + k["east"] * lam[z][0][py]
                            new = (k["centre"] * lam[z][px][py] + along_x) + (
                                along_y[py] + diffs[1 - z] * lam[1 - z][px][py]
                            )
                            spot = plane_at(z, px, py) + x
                            dst[pl.ds(spot, 8), :] = new + seed_rows[pl.ds(seed_base + spot, 8), :]
                sums = [None] * 5
                for px in range(2):
                    c0, c1 = own[z][px]
                    mid = c1 - c0
                    to_north = (mid, jnp.where(lane == LANES - 1, 0.0, pltpu.roll(c0, LANES - 1, 1)) - c1)
                    to_south = (c0 - jnp.where(lane == 0, 0.0, pltpu.roll(c1, 1, 1)), mid)
                    for py in range(2):
                        c, l = own[z][px][py], lam[z][px][py]
                        mid_x = own[z][1][py] - own[z][0][py]
                        if px == 0:
                            to_east, to_west = mid_x, c - odd[z][py]
                        else:
                            to_east, to_west = even[z][py] - c, mid_x
                        rise = own[1 - z][px][py] - 2.0 * c
                        for q, d in enumerate((to_east, to_west, to_north[py], to_south[py], rise)):
                            term = l * d
                            sums[q] = term if sums[q] is None else sums[q] + term
                for q in range(5):
                    at = acc_at(q, z, x)
                    acc[at, :] = sums[q] if first else acc[at, :] + sums[q]
            return carry

    lams = [
        [
            [[jnp.where(patch[2] == STEPS, seed[z][px][py], 0.0) for py in range(2)] for px in range(2)]
            for z in range(2)
        ]
        for patch, seed in zip(patches, seeds)
    ]
    plume_sums = [[[zeros] * 5 for _ in range(2)] for _ in range(groups)]

    def plume_backward(t):
        for g in range(groups):
            ks, _, lasts, _, _, _, plume = patches[g]
            state, lam, seed, sums = plume[t], lams[g], seeds[g], plume_sums[g]
            new = [[[None, None], [None, None]], [[None, None], [None, None]]]
            for z in range(2):
                k = ks[z]
                for px in range(2):
                    for py in range(2):
                        c, l = state[z][px][py], lam[z][px][py]
                        c_x, c_y = state[z][1 - px][py], state[z][px][1 - py]
                        l_x, l_y = lam[z][1 - px][py], lam[z][px][1 - py]
                        if px == 0:
                            to_east, to_west = c_x - c, c - pltpu.roll(c_x, 1, 0)
                            along_x = k["west"] * l_x + pltpu.roll(k["east"] * l_x, 1, 0)
                        else:
                            to_east, to_west = pltpu.roll(c_x, 7, 0) - c, c - c_x
                            along_x = pltpu.roll(k["west"] * l_x, 7, 0) + k["east"] * l_x
                        if py == 0:
                            to_north, to_south = c_y - c, c - pltpu.roll(c_y, 1, 1)
                            along_y = k["south"] * l_y + pltpu.roll(k["north"] * l_y, 1, 1)
                        else:
                            to_north, to_south = pltpu.roll(c_y, LANES - 1, 1) - c, c - c_y
                            along_y = pltpu.roll(k["south"] * l_y, LANES - 1, 1) + k["north"] * l_y
                        rise = state[1 - z][px][py] - 2.0 * c
                        for q, d in enumerate((to_east, to_west, to_north, to_south, rise)):
                            sums[z][q] = sums[z][q] + l * d
                        value = (k["centre"] * l + along_x) + (along_y + ks[1 - z]["diff"] * lam[1 - z][px][py])
                        new[z][px][py] = value + jnp.where(lasts == t, seed[z][px][py], 0.0)
            lams[g] = new
    src, dst, src_base = seed_rows, lam_b, (STEPS - 1) * FIELD
    for t in range(STEPS - 1, -1, -1):
        if t == 0:
            backward(src, src_base, dst, 0, planes_ref, 0, False, True)
        else:
            backward(src, src_base, dst, (t - 1) * FIELD, hist, (t - 1) * FIELD, t == STEPS - 1, False)
            plume_backward(t)
        src, dst, src_base = dst, (lam_a if dst is lam_b else lam_b), 0

    def chain(sums, diff, wx, wy, fx, fy):
        to_east, to_west, to_north, to_south, rise = sums

        def wind(w, up, down, factor):
            plus = jnp.where(w > 0.0, 1.0, jnp.where(w == 0.0, 0.5, 0.0))
            return -(plus * up + (1.0 - plus) * down) * factor

        g0 = (to_east - to_west + to_north - to_south + rise) * diff
        return g0, wind(wx, to_west, to_east, fx), wind(wy, to_south, to_north, fy)

    @loop(0, ROWS // 8, unroll=16)
    def _(i, carry):
        x = pl.multiple_of(i * 8, 8)
        for z in range(2):
            sums = [acc[acc_at(q, z, x), :] for q in range(5)]
            made = chain(sums, *(coef[coef_at(name, z, x), :] for name in ("diff", "wx", "wy", "fx", "fy")))
            for f in range(3):
                grad[pl.ds((f * 2 + z) * ROWS + 8 + x, 8), :] = made[f]
        return carry

    for g in range(groups):
        members = range(g * SLOTS, min(blocks, (g + 1) * SLOTS))
        ks, valid = patches[g][:2]
        sums = plume_sums[g]
        made = []
        for z in range(2):
            k = ks[z]
            made.append(chain(sums[z], k["diff"], k["wx"], k["wy"], k["fx"], k["fy"]))
        made = [[jnp.where(valid, made[z][f], 0.0) for z in range(2)] for f in range(3)]
        for r in members:
            here = slot == r % SLOTS
            x0, y0 = about(r, 4), about(r, 5)
            shift = (y0 - 8 * (r % SLOTS)) & (LANES - 1)
            spots = [pl.ds((f * 2 + z) * ROWS + 8 + x0, 8) for f in range(3) for z in range(2)]
            news = [
                grad[spots[f * 2 + z], :] + pltpu.roll(jnp.where(here, made[f][z], 0.0), shift, 1)
                for f in range(3)
                for z in range(2)
            ]
            for spot, new in zip(spots, news):
                grad[spot, :] = new

    power = zeros
    for i in range(6 * ROWS // 8):
        g = grad[pl.ds(8 + i * 8, 8), :]
        power = power + g * g
    mean = jnp.sum(power, keepdims=True) * (1.0 / (6 * ROWS * LANES))
    scale = 1.0 / jnp.sqrt(mean + 1e-06)
    mine = me * rows + 8
    if rows % 8 == 0:
        mine = pl.multiple_of(mine, 8)
    direction_ref[...] = grad[pl.ds(mine, rows), :] * scale


def rounds(size):
    bits = [1 << i for i in range(size.bit_length() - 1)]
    return bits[2:] + bits[1::-1]


def solution(mesh):
    size = mesh.shape["rel"]
    bits = rounds(size)
    order = [0]
    for bit in bits:
        order = order + [at ^ bit for at in order]

    def local(coarse, background, sources, durations, counts, sensors, observed):
        rows = coarse.shape[0] // LANES
        block = -(-(rows + 2) // 8) * 8
        vmem = pl.BlockSpec(memory_space=pltpu.VMEM)
        smem = pl.BlockSpec(memory_space=pltpu.SMEM)
        packed = pl.pallas_call(
            pack_kernel,
            out_shape=pltpu.VMEM((block, LANES), F32),
            in_specs=[smem] * 3 + [pl.BlockSpec(memory_space=pl.ANY)] * 3,
            out_specs=vmem,
            scratch_shapes=[
                pltpu.VMEM((1, NSENS), I32),
                pltpu.VMEM((1, NSENS), F32),
                pltpu.SemaphoreType.DMA((3,)),
            ],
        )(sources, durations, counts, coarse.reshape(rows, LANES), sensors, observed)
        planes = pl.pallas_call(
            planes_kernel,
            out_shape=jax.ShapeDtypeStruct((FIELD, LANES), F32),
            in_specs=[vmem],
            out_specs=vmem,
            scratch_shapes=[pltpu.VMEM((4,) + background.shape[1:2] + (LANES,), F32)],
            compiler_params=pltpu.CompilerParams(vmem_limit_bytes=VMEM_LIMIT),
        )(background)
        held = packed.reshape(-1)
        for bit in bits:
            got = lax.ppermute(held, "rel", [(i, i ^ bit) for i in range(size)])
            if bit != bits[-1]:
                own = lax.optimization_barrier(jnp.concatenate([held, jnp.zeros_like(held)]))
                held = lax.optimization_barrier(lax.dynamic_update_slice(own, got, (held.shape[0],)))
        direction, misfit = pl.pallas_call(
            functools.partial(gradient_kernel, order, rows),
            out_shape=(jax.ShapeDtypeStruct((rows, LANES), F32), jax.ShapeDtypeStruct((1,), F32)),
            in_specs=[vmem, vmem, vmem],
            out_specs=(vmem, smem),
            scratch_shapes=[
                pltpu.VMEM((6 * ROWS + 16, LANES), F32),
                pltpu.VMEM((14 * 2 * PLANE, LANES), F32),
                pltpu.VMEM((STEPS * FIELD, LANES), F32),
                pltpu.VMEM((FIELD, LANES), F32),
                pltpu.VMEM((FIELD, LANES), F32),
                pltpu.VMEM((10 * ROWS, LANES), F32),
                pltpu.VMEM((6 * ROWS + 16, LANES), F32),
                pltpu.VMEM((size, LANES), F32),
                pltpu.VMEM((size, LANES), F32),
                pltpu.VMEM((size // 2 + size, LANES), I32),
                pltpu.VMEM((size * NSENS, LANES), F32),
                pltpu.VMEM((size * NSENS, LANES), F32),
                pltpu.VMEM((STEPS * FIELD, LANES), F32),
                pltpu.VMEM((2 * size, LANES), I32),
                pltpu.VMEM((size + 8, LANES), F32),
                pltpu.VMEM((-(-size // SLOTS) * LANES, LANES), BF16),
                pltpu.VMEM((-(-size // SLOTS) * LANES, LANES), F32),
                pltpu.SMEM((size // 2 + size, LANES), I32),
                pltpu.SemaphoreType.DMA,
            ],
            compiler_params=pltpu.CompilerParams(vmem_limit_bytes=VMEM_LIMIT),
        )(held.reshape(-1, LANES), got.reshape(-1, LANES), planes)
        return direction.reshape(-1), misfit

    in_specs = (
        P(("grp", "rel")),
        P("grp", None, None),
        P(("grp", "rel")),
        P(("grp", "rel")),
        P(("grp", "rel")),
        P(("grp", "rel"), None),
        P(("grp", "rel"), None),
    )
    out_specs = (P(("grp", "rel")), P(("grp", "rel")))
    return jax.shard_map(local, mesh=mesh, in_specs=in_specs, out_specs=out_specs, check_vma=False)
```

```python
import functools

import jax
import jax.numpy as jnp
from jax import lax
from jax.experimental import pallas as pl
from jax.experimental.pallas import tpu as pltpu
from jax.sharding import PartitionSpec as P

STEPS = 6
NSENS = 64
PAD = 8
BATCH = 16
SLOTS = 16
PAIRS = SLOTS // 2
ROWS = 128
LANES = 128
PLANE = ROWS + 2 * PAD
FIELD = 8 * PLANE
VMEM_LIMIT = 40 * 1024 * 1024
F32, BF16, I32 = jnp.float32, jnp.bfloat16, jnp.int32


def loop(first, end, unroll=None):
    def run(body):
        lax.fori_loop(first, end, body, None, unroll=unroll)

    return run


def plane_at(z, px, py):
    return ((z * 2 + px) * 2 + py) * PLANE + PAD


def split(value):
    high = value.astype(BF16)
    return high, (value - high.astype(F32)).astype(BF16)


def pack_kernel(source_ref, duration_ref, count_ref, coarse_ref, sensors_ref, observed_ref, out_ref, *rest):
    sensors, observed, sems = rest
    rows = coarse_ref.shape[0]
    pairs = ((coarse_ref, out_ref.at[pl.ds(0, rows), :]), (sensors_ref, sensors), (observed_ref, observed))
    copies = [pltpu.make_async_copy(src, dst, sems.at[i]) for i, (src, dst) in enumerate(pairs)]
    for copy in copies:
        copy.start()
    lane = lax.broadcasted_iota(I32, (1, LANES), 1)
    record = jnp.where(lane == 0, source_ref[0], jnp.where(lane == 1, duration_ref[0], count_ref[0]))
    for copy in copies:
        copy.wait()
    out_ref[pl.ds(rows, 1), pl.ds(0, NSENS)] = sensors[...].astype(F32)
    out_ref[pl.ds(rows, 1), pl.ds(NSENS, NSENS)] = observed[...]
    out_ref[pl.ds(rows + 1, 1), :] = record.astype(F32)
    spare = out_ref.shape[0] - rows - 2
    out_ref[pl.ds(rows + 2, spare), :] = jnp.zeros((spare, LANES), F32)


def planes_kernel(background_ref, out_ref, half_ref):
    width = background_ref.shape[2]
    out_ref[...] = jnp.zeros_like(out_ref)
    column = lax.broadcasted_iota(I32, (width, width), 1)
    row = lax.broadcasted_iota(I32, (width, width), 0)
    wanted = jnp.where(column < LANES, 2 * column, 2 * (column - LANES) + 1)
    pick = (row == wanted).astype(F32)
    for z in range(2):
        sorted_lanes = jnp.dot(
            background_ref[z], pick, precision=lax.Precision.HIGHEST, preferred_element_type=F32
        )
        for py in range(2):
            half_ref[z * 2 + py] = sorted_lanes[:, py * LANES : (py + 1) * LANES]
            for px in range(2):
                out_ref[pl.ds(plane_at(z, px, py), ROWS), :] = half_ref[z * 2 + py, pl.ds(px, ROWS, stride=2), :]


def gradient_kernel(
    order,
    rows,
    first_ref,
    second_ref,
    planes_ref,
    direction_ref,
    misfit_ref,
    par,
    coef,
    hist,
    lam_a,
    lam_b,
    acc,
    grad,
    sens_rows,
    meta_rows,
    table,
    gathered,
    scattered,
    seed_rows,
    sensor_ints,
    sensor_reals,
    flats,
    patch_seeds,
    slope_lap,
    slope_x,
    slope_y,
    scalars,
    sem,
):
    blocks = len(order)
    block = first_ref.shape[0] // (blocks // 2)
    me = lax.axis_index("rel")
    half = blocks // 2
    slopes = (slope_lap, slope_x, slope_y)
    groups = -(-half // PAIRS)
    lane = lax.broadcasted_iota(I32, (8, LANES), 1)
    sub = lax.broadcasted_iota(I32, (8, LANES), 0)

    par[pl.ds(0, 8), :] = jnp.zeros((8, LANES), F32)
    par[pl.ds(8 + 6 * ROWS, 8), :] = jnp.zeros((8, LANES), F32)
    for p in range(blocks):
        ref = first_ref if p < blocks // 2 else second_ref
        at = (p % (blocks // 2)) * block
        owner = me ^ order[p]
        if rows % 8 == 0:
            place = pl.multiple_of(owner * rows + 8, 8)
        else:
            place = owner * rows + 8
        par[pl.ds(place, rows), :] = ref[pl.ds(at, rows), :]
        stand = (owner // SLOTS) * PAIRS + owner % PAIRS + ((owner // PAIRS) % 2) * half
        sens_rows[pl.ds(stand, 1), :] = ref[pl.ds(at + rows, 1), :]
        meta_rows[pl.ds(stand, 1), :] = ref[pl.ds(at + rows + 1, 1), :]

    wide = lax.broadcasted_iota(I32, (blocks, LANES), 1)
    place = lax.broadcasted_iota(I32, (blocks, LANES), 0)
    meta = meta_rows[...].astype(I32)

    pair_lane, pair_row = wide[:half], place[:half]
    first = pair_lane < NSENS

    def paired(value):
        return jnp.where(first, value[:half], value[half:])

    def spread(value):
        return jnp.broadcast_to(value, (blocks, LANES))

    straight = sens_rows[...]
    turned = pltpu.roll(straight, NSENS, 1)
    sens = jnp.where(first, straight[:half], turned[half:]).astype(I32)
    watched = jnp.where(first, turned[:half], straight[half:])
    source, count = spread(meta[:, 0:1]), spread(meta[:, 2:3])
    left_x = (((source >> 8) & 255) >> 1) - 3
    left_y = ((source & 255) >> 1) - 3
    fine_x, fine_y = (sens >> 8) & 255, sens & 255
    plane = (sens >> 16) * 4 + (fine_x & 1) * 2 + (fine_y & 1)
    cell_x, cell_y = fine_x >> 1, fine_y >> 1
    off_x, off_y = cell_x - paired(left_x), cell_y - paired(left_y)
    inside = (off_x >= 0) & (off_x < 8) & (off_y >= 0) & (off_y < 8)
    slot_of = pair_row % PAIRS + jnp.where(first, 0, PAIRS)
    patch_row = jnp.where(inside, plane * 8 + off_x, -1)
    patch_lane = jnp.where(inside, slot_of * 8 + off_y, -1)
    address = plane * PLANE + PAD + cell_x
    for at, value in ((4, left_x), (5, left_y)):
        meta = jnp.where(wide == at, value, meta)
    table[pl.ds(0, half), :] = address + (paired(count) - 1) * FIELD
    table[pl.ds(half, blocks), :] = meta
    copy = pltpu.make_async_copy(table, scalars, sem)
    copy.start()
    sensor_reals[pl.ds(0, half), :] = watched
    sensor_reals[pl.ds(half, half), :] = ((pair_row // PAIRS) * SLOTS + slot_of == me).astype(F32)
    for i, value in enumerate((cell_y, patch_lane, patch_row, address)):
        sensor_ints[pl.ds(i * half, half), :] = value

    def about(j, lane_at):
        return scalars[half + (j // SLOTS) * PAIRS + j % PAIRS + (j // PAIRS % 2) * half, lane_at]

    names = ("centre", "east", "west", "north", "south", "diff", "up_x", "up_y", "northr", "southl", "wx", "wy", "fx", "fy")
    index = {name: i for i, name in enumerate(names)}

    def coef_at(name, z, x):
        return pl.ds((index[name] * 2 + z) * PLANE + PAD + x, 8)

    zeros = jnp.zeros((8, LANES), F32)
    for z in range(2):
        coef[coef_at("east", z, -8), :] = zeros
        coef[coef_at("west", z, ROWS), :] = zeros

    def share(w):
        return jnp.where(w > 0.0, 1.0, jnp.where(w == 0.0, 0.5, 0.0))

    def coefficients(p0, p1, p2):
        diff = 0.05 * jnp.exp(p0)
        t1, t2 = jnp.tanh(p1), jnp.tanh(p2)
        wx, wy = 0.08 * t1, 0.08 * t2
        east, west = diff - jnp.minimum(wx, 0.0), diff + jnp.maximum(wx, 0.0)
        north, south = diff - jnp.minimum(wy, 0.0), diff + jnp.maximum(wy, 0.0)
        centre = 1.0 - (east + west + north + south + 2.0 * diff)
        return dict(
            centre=centre, east=east, west=west, north=north, south=south, diff=diff,
            wx=wx, wy=wy, fx=0.08 * (1.0 - t1 * t1), fy=0.08 * (1.0 - t2 * t2),
        )

    @loop(0, ROWS // 8, unroll=16)
    def _(i, carry):
        x = pl.multiple_of(i * 8, 8)
        for z in range(2):
            p0, p1, p2 = (par[pl.ds((f * 2 + z) * ROWS + 8 + x, 8), :] for f in range(3))
            made = coefficients(p0, p1, p2)
            made["up_x"], made["up_y"] = share(made["wx"]), share(made["wy"])
            made["northr"] = jnp.where(lane == 0, 0.0, pltpu.roll(made["north"], 1, 1))
            made["southl"] = jnp.where(lane == LANES - 1, 0.0, pltpu.roll(made["south"], LANES - 1, 1))
            for name, value in made.items():
                coef[coef_at(name, z, x), :] = value
        return carry

    for p in range(8):
        for ref, fields in ((hist, STEPS), (seed_rows, STEPS), (lam_a, 1), (lam_b, 1)):
            for f in range(fields):
                ref[pl.ds(f * FIELD + p * PLANE, 8), :] = zeros
                ref[pl.ds(f * FIELD + p * PLANE + PAD + ROWS, 8), :] = zeros

    def load(ref, base, x):
        def at(z, px, py, shift=0):
            return ref[pl.ds(base + plane_at(z, px, py) + x + shift, 8), :]

        own = [[[at(z, px, py) for py in range(2)] for px in range(2)] for z in range(2)]
        odd = [[at(z, 1, py, -1) for py in range(2)] for z in range(2)]
        even = [[at(z, 0, py, 1) for py in range(2)] for z in range(2)]
        return own, odd, even

    def forward(src, src_base, dst, dst_base):
        @loop(0, ROWS // 8, unroll=16)
        def _(i, carry):
            x = pl.multiple_of(i * 8, 8)
            own, odd, even = load(src, src_base, x)
            for z in range(2):
                k = {name: coef[coef_at(name, z, x), :] for name in ("diff", "wx", "wy", "up_x", "up_y")}
                to_x, lap_x = [None] * 2, [None] * 2
                for py in range(2):
                    c0, c1 = own[z][0][py], own[z][1][py]
                    mid, east = c1 - c0, even[z][py] - c1
                    to_x[py] = (mid, east)
                    lap_x[py] = (mid - (c0 - odd[z][py]), east - mid)
                for px in range(2):
                    c0, c1 = own[z][px]
                    mid = c1 - c0
                    north = jnp.where(lane == LANES - 1, 0.0, pltpu.roll(c0, LANES - 1, 1)) - c1
                    south = c0 - jnp.where(lane == 0, 0.0, pltpu.roll(c1, 1, 1))
                    to_y, lap_y = (mid, north), (mid - south, north - mid)
                    for py in range(2):
                        c = own[z][px][py]
                        lap = (lap_x[py][px] + lap_y[py]) + ((own[1 - z][px][py] - c) - c)
                        up_x = to_x[py][px] - k["up_x"] * lap_x[py][px]
                        up_y = to_y[py] - k["up_y"] * lap_y[py]
                        at = pl.ds(dst_base + plane_at(z, px, py) + x, 8)
                        dst[at, :] = (c + k["diff"] * lap) - (k["wx"] * up_x + k["wy"] * up_y)
                        seed_rows[at, :] = zeros
                        for ref, value in zip(slopes, (lap, up_x, up_y)):
                            ref[at, :] = value

    copy.wait()

    slot = lane >> 3
    patches = []
    for g in range(groups):
        members = range(g * SLOTS, min(blocks, (g + 1) * SLOTS))
        pp = [[zeros, zeros] for _ in range(3)]
        at_x, at_y, of_plane, lasts, emits = (jnp.zeros((8, LANES), I32) for _ in range(5))
        for r in members:
            here = slot == r % SLOTS
            src, dur, cnt, x0, y0 = (about(r, at) for at in (0, 1, 2, 4, 5))
            shift = (8 * (r % SLOTS) - y0) & (LANES - 1)
            for f in range(3):
                for z in range(2):
                    window = par[pl.ds((f * 2 + z) * ROWS + 8 + x0, 8), :]
                    pp[f][z] = jnp.where(here, pltpu.roll(window, shift, 1), pp[f][z])
            src_plane = (src >> 16) * 4 + ((src >> 8) & 1) * 2 + (src & 1)
            at_x = jnp.where(here, x0, at_x)
            at_y = jnp.where(here, y0, at_y)
            of_plane = jnp.where(here, src_plane, of_plane)
            emits = jnp.where(here, dur, emits)
            lasts = jnp.where(here, cnt, lasts)
        in_x, in_y = at_x + sub, at_y + (lane & 7)
        valid = (in_x >= 0) & (in_x < ROWS) & (in_y >= 0) & (in_y < LANES)
        ks = []
        for z in range(2):
            made = coefficients(pp[0][z], pp[1][z], pp[2][z])
            ks.append({name: jnp.where(valid, value, 0.0) for name, value in made.items()})
        spot = (sub == 3) & ((lane & 7) == 3)
        state = [[[zeros for _ in range(2)] for _ in range(2)] for _ in range(2)]
        patches.append((ks, valid, lasts, of_plane, emits, spot, [state]))

    def plume_forward(t):
        for ks, _, lasts, of_plane, emits, spot, plume in patches:
            state = plume[t]
            new = [[[None, None], [None, None]], [[None, None], [None, None]]]
            for z in range(2):
                k = ks[z]
                for px in range(2):
                    for py in range(2):
                        c = state[z][px][py]
                        other_x, other_y = state[z][1 - px][py], state[z][px][1 - py]
                        if px == 0:
                            along_x = k["east"] * other_x + k["west"] * pltpu.roll(other_x, 1, 0)
                        else:
                            along_x = k["east"] * pltpu.roll(other_x, 7, 0) + k["west"] * other_x
                        if py == 0:
                            along_y = k["north"] * other_y + k["south"] * pltpu.roll(other_y, 1, 1)
                        else:
                            along_y = k["north"] * pltpu.roll(other_y, LANES - 1, 1) + k["south"] * other_y
                        value = (k["centre"] * c + along_x) + (along_y + k["diff"] * state[1 - z][px][py])
                        emit = spot & (of_plane == z * 4 + px * 2 + py) & (t < emits)
                        value = value + jnp.where(emit, 4.0, 0.0)
                        new[z][px][py] = jnp.where(t < lasts, value, c)
            plume.append(new)

    for t in range(STEPS):
        plume_forward(t)
        if t == 0:
            forward(planes_ref, 0, hist, 0)
        else:
            forward(hist, (t - 1) * FIELD, hist, t * FIELD)

    def with_rows(a, b):
        return lax.dot_general(a, b, (((1,), (1,)), ((), ())), preferred_element_type=F32)

    sub_sq = lax.broadcasted_iota(I32, (LANES, LANES), 0)
    lane_sq = lax.broadcasted_iota(I32, (LANES, LANES), 1)
    diagonal = sub_sq == lane_sq
    batch = (lane_sq // BATCH) == (sub_sq // BATCH)
    for g in range(groups):
        final = patches[g][-1][STEPS]
        flat = jnp.concatenate([final[z][px][py] for z in range(2) for px in range(2) for py in range(2)], axis=0)
        flats[pl.ds(g * LANES, LANES), :] = jnp.concatenate(split(flat), axis=0)
        patch_seeds[pl.ds(g * LANES, LANES), :] = jnp.zeros((LANES, LANES), F32)
    misfit_row = sensor_reals.at[pl.ds(2 * half, 1), :]
    misfit_row[...] = jnp.zeros((1, LANES), F32)

    def read_rows(j, part):
        to = pl.multiple_of(j * LANES, LANES)
        for s in range(part * BATCH, (part + 1) * BATCH):
            gathered[pl.ds(to + s, 1), :] = hist[pl.ds(scalars[j, s], 1), :]

    def add_rows(j, part):
        to = pl.multiple_of(j * LANES, LANES)
        spots = [pl.ds(scalars[j, s], 1) for s in range(part * BATCH, (part + 1) * BATCH)]
        news = [seed_rows[spot, :] + scattered[pl.ds(to + part * BATCH + s, 1), :] for s, spot in enumerate(spots)]
        for spot, new in zip(spots, news):
            seed_rows[spot, :] = new

    def row_of(i, j):
        return jnp.broadcast_to(sensor_ints[pl.ds(i * half + j, 1), :], (LANES, LANES))

    def group_of(j):
        return pl.ds(pl.multiple_of(j // PAIRS * LANES, LANES), LANES)

    def values_of(j):
        at_lane = (sub_sq == row_of(0, j)).astype(F32).astype(BF16)
        at_patch = (sub_sq == row_of(1, j)).astype(F32).astype(BF16)
        put = sub_sq[:NSENS] == row_of(2, j)[:NSENS]
        high, low = split(gathered[pl.ds(pl.multiple_of(j * LANES, LANES), LANES), :])
        far = jnp.dot(high, at_lane, preferred_element_type=F32) + jnp.dot(low, at_lane, preferred_element_type=F32)
        near = jnp.dot(flats[group_of(j), :], at_patch, preferred_element_type=F32)
        return at_lane, at_patch, put, far, near

    def residuals_of(j, at_lane, at_patch, put, far, near):
        far = jnp.sum(jnp.where(diagonal, far, 0.0), axis=0, keepdims=True)
        near = jnp.sum(jnp.where(put, near[:NSENS] + near[NSENS:], 0.0), axis=0, keepdims=True)
        residual = far + near - sensor_reals[pl.ds(j, 1), :]
        misfit_row[...] += sensor_reals[pl.ds(half + j, 1), :] * residual * residual
        row_id = row_of(3, j).astype(F32)
        same = (row_id == row_id.T) & batch
        return residual, same, at_lane, at_patch, put

    def seeds_of(j, residual, same, at_lane, at_patch, put):
        high, low = split(jnp.where(same, jnp.broadcast_to(residual, (LANES, LANES)), 0.0))
        to = pl.multiple_of(j * LANES, LANES)
        scattered[pl.ds(to, LANES), :] = with_rows(high, at_lane) + with_rows(low, at_lane)
        put = jnp.where(put, jnp.broadcast_to(residual, (NSENS, LANES)), 0.0)
        patch_seeds[group_of(j), :] += with_rows(jnp.concatenate(split(put), axis=0), at_patch)

    @loop(0, groups, unroll=groups == 1)
    def _(g, carry):
        made = {}
        for i in range(PAIRS + 2):
            for part in range(LANES // BATCH):
                if i < PAIRS:
                    read_rows(g * PAIRS + i, part)
                if i >= 2:
                    add_rows(g * PAIRS + i - 2, part)
                if 1 <= i <= PAIRS:
                    j = g * PAIRS + i - 1
                    if part == 0:
                        made[i] = values_of(j)
                    elif part == 1:
                        made[i] = residuals_of(j, *made[i])
                    elif part == 2:
                        seeds_of(j, *made[i])

    seeds = []
    for g in range(groups):
        seed = patch_seeds[pl.ds(g * LANES, NSENS), :] + patch_seeds[pl.ds(g * LANES + NSENS, NSENS), :]
        seeds.append(
            [[[seed[((z * 2 + px) * 2 + py) * 8 :][:8] for py in range(2)] for px in range(2)] for z in range(2)]
        )
    misfit_ref[0] = jnp.sum(misfit_row[...]) * (0.5 / NSENS)

    def acc_at(q, z, x):
        return pl.ds((q * 2 + z) * ROWS + x, 8)

    def backward(src, src_base, dst, seed_base, slope_base, first, last):
        @loop(0, ROWS // 8, unroll=16)
        def _(i, carry):
            x = pl.multiple_of(i * 8, 8)
            lam, lam_odd, lam_even = load(src, src_base, x)
            diffs = [coef[coef_at("diff", z, x), :] for z in range(2)]
            for z in range(2):
                if not last:
                    k = {
                        name: coef[coef_at(name, z, x), :]
                        for name in ("centre", "east", "west", "north", "south", "northr", "southl")
                    }
                    east_m, west_p = coef[coef_at("east", z, x - 1), :], coef[coef_at("west", z, x + 1), :]
                    for px in range(2):
                        l0, l1 = lam[z][px]
                        along_y = (
                            k["south"] * l1 + k["northr"] * pltpu.roll(l1, 1, 1),
                            k["southl"] * pltpu.roll(l0, LANES - 1, 1) + k["north"] * l0,
                        )
                        for py in range(2):
                            if px == 0:
                                along_x = k["west"] * lam[z][1][py] + east_m * lam_odd[z][py]
                            else:
                                along_x = west_p * lam_even[z][py] + k["east"] * lam[z][0][py]
                            new = (k["centre"] * lam[z][px][py] + along_x) + (
                                along_y[py] + diffs[1 - z] * lam[1 - z][px][py]
                            )
                            spot = plane_at(z, px, py) + x
                            dst[pl.ds(spot, 8), :] = new + seed_rows[pl.ds(seed_base + spot, 8), :]
                sums = [None] * 3
                for px in range(2):
                    for py in range(2):
                        at = pl.ds(slope_base + plane_at(z, px, py) + x, 8)
                        for q, ref in enumerate(slopes):
                            term = lam[z][px][py] * ref[at, :]
                            sums[q] = term if sums[q] is None else sums[q] + term
                for q in range(3):
                    at = acc_at(q, z, x)
                    acc[at, :] = sums[q] if first else acc[at, :] + sums[q]

    lams = [
        [
            [[jnp.where(patch[2] == STEPS, seed[z][px][py], 0.0) for py in range(2)] for px in range(2)]
            for z in range(2)
        ]
        for patch, seed in zip(patches, seeds)
    ]
    plume_sums = [[[zeros] * 5 for _ in range(2)] for _ in range(groups)]

    def plume_backward(t):
        for g in range(groups):
            ks, _, lasts, _, _, _, plume = patches[g]
            state, lam, seed, sums = plume[t], lams[g], seeds[g], plume_sums[g]
            new = [[[None, None], [None, None]], [[None, None], [None, None]]]
            for z in range(2):
                k = ks[z]
                for px in range(2):
                    for py in range(2):
                        c, l = state[z][px][py], lam[z][px][py]
                        c_x, c_y = state[z][1 - px][py], state[z][px][1 - py]
                        l_x, l_y = lam[z][1 - px][py], lam[z][px][1 - py]
                        if px == 0:
                            to_east, to_west = c_x - c, c - pltpu.roll(c_x, 1, 0)
                            along_x = k["west"] * l_x + pltpu.roll(k["east"] * l_x, 1, 0)
                        else:
                            to_east, to_west = pltpu.roll(c_x, 7, 0) - c, c - c_x
                            along_x = pltpu.roll(k["west"] * l_x, 7, 0) + k["east"] * l_x
                        if py == 0:
                            to_north, to_south = c_y - c, c - pltpu.roll(c_y, 1, 1)
                            along_y = k["south"] * l_y + pltpu.roll(k["north"] * l_y, 1, 1)
                        else:
                            to_north, to_south = pltpu.roll(c_y, LANES - 1, 1) - c, c - c_y
                            along_y = pltpu.roll(k["south"] * l_y, LANES - 1, 1) + k["north"] * l_y
                        rise = state[1 - z][px][py] - 2.0 * c
                        for q, d in enumerate((to_east, to_west, to_north, to_south, rise)):
                            sums[z][q] = sums[z][q] + l * d
                        value = (k["centre"] * l + along_x) + (along_y + ks[1 - z]["diff"] * lam[1 - z][px][py])
                        new[z][px][py] = value + jnp.where(lasts == t, seed[z][px][py], 0.0)
            lams[g] = new
    src, dst, src_base = seed_rows, lam_b, (STEPS - 1) * FIELD
    for t in range(STEPS - 1, -1, -1):
        if t == 0:
            backward(src, src_base, dst, 0, 0, False, True)
        else:
            backward(src, src_base, dst, (t - 1) * FIELD, t * FIELD, t == STEPS - 1, False)
            plume_backward(t)
        src, dst, src_base = dst, (lam_a if dst is lam_b else lam_b), 0

    def chain(sums, diff, wx, wy, fx, fy):
        to_east, to_west, to_north, to_south, rise = sums

        def wind(w, up, down, factor):
            plus = share(w)
            return -(plus * up + (1.0 - plus) * down) * factor

        g0 = (to_east - to_west + to_north - to_south + rise) * diff
        return g0, wind(wx, to_west, to_east, fx), wind(wy, to_south, to_north, fy)

    @loop(0, ROWS // 8, unroll=16)
    def _(i, carry):
        x = pl.multiple_of(i * 8, 8)
        for z in range(2):
            signed = (("diff", 1.0), ("fx", -1.0), ("fy", -1.0))
            for f, (name, sign) in enumerate(signed):
                made = acc[acc_at(f, z, x), :] * (sign * coef[coef_at(name, z, x), :])
                grad[pl.ds((f * 2 + z) * ROWS + 8 + x, 8), :] = made

    for g in range(groups):
        members = range(g * SLOTS, min(blocks, (g + 1) * SLOTS))
        ks, valid = patches[g][:2]
        sums = plume_sums[g]
        made = []
        for z in range(2):
            k = ks[z]
            made.append(chain(sums[z], k["diff"], k["wx"], k["wy"], k["fx"], k["fy"]))
        made = [[jnp.where(valid, made[z][f], 0.0) for z in range(2)] for f in range(3)]
        for r in members:
            here = slot == r % SLOTS
            x0, y0 = about(r, 4), about(r, 5)
            shift = (y0 - 8 * (r % SLOTS)) & (LANES - 1)
            spots = [pl.ds((f * 2 + z) * ROWS + 8 + x0, 8) for f in range(3) for z in range(2)]
            news = [
                grad[spots[f * 2 + z], :] + pltpu.roll(jnp.where(here, made[f][z], 0.0), shift, 1)
                for f in range(3)
                for z in range(2)
            ]
            for spot, new in zip(spots, news):
                grad[spot, :] = new

    power = zeros
    for i in range(6 * ROWS // 8):
        g = grad[pl.ds(8 + i * 8, 8), :]
        power = power + g * g
    mean = jnp.sum(power, keepdims=True) * (1.0 / (6 * ROWS * LANES))
    scale = 1.0 / jnp.sqrt(mean + 1e-06)
    mine = me * rows + 8
    if rows % 8 == 0:
        mine = pl.multiple_of(mine, 8)
    direction_ref[...] = grad[pl.ds(mine, rows), :] * scale


def rounds(size):
    bits = [1 << i for i in range(size.bit_length() - 1)]
    return bits[2:] + bits[1::-1]


def solution(mesh):
    size = mesh.shape["rel"]
    bits = rounds(size)
    order = [0]
    for bit in bits:
        order = order + [at ^ bit for at in order]

    def local(coarse, background, sources, durations, counts, sensors, observed):
        rows = coarse.shape[0] // LANES
        block = -(-(rows + 2) // 8) * 8
        vmem = pl.BlockSpec(memory_space=pltpu.VMEM)
        smem = pl.BlockSpec(memory_space=pltpu.SMEM)
        packed = pl.pallas_call(
            pack_kernel,
            out_shape=pltpu.VMEM((block, LANES), F32),
            in_specs=[smem] * 3 + [pl.BlockSpec(memory_space=pl.ANY)] * 3,
            out_specs=vmem,
            scratch_shapes=[
                pltpu.VMEM((1, NSENS), I32),
                pltpu.VMEM((1, NSENS), F32),
                pltpu.SemaphoreType.DMA((3,)),
            ],
        )(sources, durations, counts, coarse.reshape(rows, LANES), sensors, observed)
        planes = pl.pallas_call(
            planes_kernel,
            out_shape=jax.ShapeDtypeStruct((FIELD, LANES), F32),
            in_specs=[vmem],
            out_specs=vmem,
            scratch_shapes=[pltpu.VMEM((4,) + background.shape[1:2] + (LANES,), F32)],
            compiler_params=pltpu.CompilerParams(vmem_limit_bytes=VMEM_LIMIT),
        )(background)
        held = packed.reshape(-1)
        for bit in bits:
            got = lax.ppermute(held, "rel", [(i, i ^ bit) for i in range(size)])
            if bit != bits[-1]:
                own = lax.optimization_barrier(jnp.concatenate([held, jnp.zeros_like(held)]))
                held = lax.optimization_barrier(lax.dynamic_update_slice(own, got, (held.shape[0],)))
        direction, misfit = pl.pallas_call(
            functools.partial(gradient_kernel, order, rows),
            out_shape=(jax.ShapeDtypeStruct((rows, LANES), F32), jax.ShapeDtypeStruct((1,), F32)),
            in_specs=[vmem, vmem, vmem],
            out_specs=(vmem, smem),
            scratch_shapes=[
                pltpu.VMEM((6 * ROWS + 16, LANES), F32),
                pltpu.VMEM((14 * 2 * PLANE, LANES), F32),
                pltpu.VMEM((STEPS * FIELD, LANES), F32),
                pltpu.VMEM((FIELD, LANES), F32),
                pltpu.VMEM((FIELD, LANES), F32),
                pltpu.VMEM((6 * ROWS, LANES), F32),
                pltpu.VMEM((6 * ROWS + 16, LANES), F32),
                pltpu.VMEM((size, LANES), F32),
                pltpu.VMEM((size, LANES), F32),
                pltpu.VMEM((size // 2 + size, LANES), I32),
                pltpu.VMEM((size * NSENS, LANES), F32),
                pltpu.VMEM((size * NSENS, LANES), F32),
                pltpu.VMEM((STEPS * FIELD, LANES), F32),
                pltpu.VMEM((2 * size, LANES), I32),
                pltpu.VMEM((size + 8, LANES), F32),
                pltpu.VMEM((-(-size // SLOTS) * LANES, LANES), BF16),
                pltpu.VMEM((-(-size // SLOTS) * LANES, LANES), F32),
                pltpu.VMEM((STEPS * FIELD, LANES), F32),
                pltpu.VMEM((STEPS * FIELD, LANES), F32),
                pltpu.VMEM((STEPS * FIELD, LANES), F32),
                pltpu.SMEM((size // 2 + size, LANES), I32),
                pltpu.SemaphoreType.DMA,
            ],
            compiler_params=pltpu.CompilerParams(vmem_limit_bytes=VMEM_LIMIT),
        )(held.reshape(-1, LANES), got.reshape(-1, LANES), planes)
        return direction.reshape(-1), misfit

    in_specs = (
        P(("grp", "rel")),
        P("grp", None, None),
        P(("grp", "rel")),
        P(("grp", "rel")),
        P(("grp", "rel")),
        P(("grp", "rel"), None),
        P(("grp", "rel"), None),
    )
    out_specs = (P(("grp", "rel")), P(("grp", "rel")))
    return jax.shard_map(local, mesh=mesh, in_specs=in_specs, out_specs=out_specs, check_vma=False)
```
